512 devices in a mesh: samp: 8 (over x, core), field: 64 (over y, z).
Axes of the slice: x: 4, y: 4, z: 16, core: 2. Of those that a mesh axis runs over, the one named last changes fastest.
Arguments:
- mean_start: float32 [128, 128, 256], P('field'), may hold values from -3 to 3
- sample_draws: float32 [4, 128, 128, 256], P(None, 'field'), may hold values from -3 to 3
- kernel: float32 [3, 256], replicated, may hold values from 0.15 to 0.35
- sight_mask: int32 [128, 128], P('field'), may hold values 0 or 1
- noise_weight: float32 [128, 128], P('field'), may hold values from 0.2 to 5
- data: float32 [128, 128], P('field'), may hold values from 0.6 to 1.6
Outputs:
- mean_final: float32 [128, 128, 256], P('field')
- cg_residual: float32 [128, 128, 256], P('field')
The draws below stay inside these ranges and needn't reach their ends.
All inputs are finite; a program needn't handle non-finite values. No bound on the sum of `sight_mask` on one device may be relied on, other than what follows from the above.
Results may differ from the reference program's by a relative error of at most 0.0065.
Values sent between devices are 32-bit elements; how exact they have to be, the bound alone decides.
No kernel may reach another device: no remote copies, remote signals or barrier semaphores. Data moves between devices by JAX's collectives and lax.ppermute only.
A program may use at most 64 MiB of HBM per device.

```python
import math
import jax
import jax.numpy as jnp
from jax import lax

NY = 128
NZ = 256
NEWTON = 2
ITERS = 3
NX = 128
SAMPLES = 8
PAIRS = 4


def plant(result, stream_key, smallest, largest):
    longest = result.shape.index(max(result.shape))
    spots = []
    for shift in (0, 1):
        where = [jax.random.randint(jax.random.fold_in(stream_key, axis), (), 0, length) for axis, length in enumerate(result.shape)]
        where[longest] = (where[longest] + shift) % result.shape[longest]
        spots.append(tuple(where))
    return result.at[spots[0]].set(smallest).at[spots[1]].set(largest)


def levels(stream_key, extent, pieces, smallest, largest):
    factor_of, own = 1.0, jax.random.fold_in(stream_key, 6)
    for axis_at, shards_of in pieces:
        heights = jnp.exp(jax.random.uniform(jax.random.fold_in(own, axis_at), (shards_of,), jnp.float32, smallest / len(pieces), largest / len(pieces)))
        factor_of = factor_of * jnp.repeat(heights, extent[axis_at] // shards_of).reshape([-1 if axis == axis_at else 1 for axis in range(len(extent))])
    return factor_of


def centred(rng, extent, deviation, limit, cuts=(), held_as=jnp.bfloat16):
    result = deviation * jax.random.normal(rng, extent, jnp.float32)
    if cuts:
        result = result * levels(rng, extent, cuts, -0.22, 0.18)
    return jnp.clip(result, -limit, limit).astype(held_as)


def setup_inputs(seed: int = 0) -> dict:
    seeds = jax.random.split(jax.random.key(seed), 7)
    mean_start = centred(seeds[0], (NX, NY, NZ), 0.25, 3.0, ((0, 64),), jnp.float32)
    sample_draws = centred(seeds[1], (PAIRS, NX, NY, NZ), 0.25, 3.0, ((1, 64),), jnp.float32)
    kernel = jnp.clip(jax.random.uniform(seeds[2], (3, NZ), jnp.float32, 0.15, 0.35), 0.15, 0.35)
    sight_mask = plant((jax.random.randint(seeds[3], (NX, NY), 0, 4) < 3).astype(jnp.int32), jax.random.fold_in(seeds[3], 1), 0, 1)
    noise_weight = jnp.clip(jnp.exp(math.log(5.0) - 3.218876 * jax.random.uniform(seeds[4], (NX, NY), jnp.float32) ** levels(seeds[4], (NX, NY), ((0, 64),), -0.2, 0.2)), 0.2, 5.0)
    data = jnp.clip(0.6 + 1.0 * jax.random.uniform(seeds[5], (NX, NY), jnp.float32) ** levels(seeds[5], (NX, NY), ((0, 64),), -0.2, 0.2), 0.6, 1.6)
    return {"mean_start": mean_start, "sample_draws": sample_draws, "kernel": kernel, "sight_mask": sight_mask, "noise_weight": noise_weight, "data": data}


def refine(v, kernel):
    padded = jnp.pad(v, ((1, 1), (0, 0), (0, 0)))
    return kernel[0] * padded[:-2] + kernel[1] * padded[1:-1] + kernel[2] * padded[2:]

def transpose_refine(u, kernel):
    padded = jnp.pad(u, ((1, 1), (0, 0), (0, 0)))
    return kernel[0] * padded[2:] + kernel[1] * padded[1:-1] + kernel[2] * padded[:-2]

def reference(mean_start, sample_draws, kernel, sight_mask, noise_weight, data):
    scale_q = 1.0 / jnp.sqrt(jnp.float32(NZ))
    maskf = sight_mask.astype(jnp.float32)
    latent = mean_start
    residual = mean_start
    for outer in range(NEWTON):
        signals = []
        for index in range(SAMPLES):
            sign = 1.0 if index % 2 == 0 else -1.0
            signals.append(jnp.exp(refine(latent + sign * sample_draws[index // 2], kernel)))
        total = jnp.zeros_like(latent)
        for signal in signals:
            error = scale_q * (maskf * lax.optimization_barrier(jnp.sum(signal, axis=2)) - NZ * data)
            total = total + signal * (maskf * noise_weight * error * scale_q)[:, :, None]
        gradient = latent + transpose_refine(total, kernel) / SAMPLES

        def metric(v):
            refined = refine(v, kernel)
            acc = jnp.zeros_like(v)
            for signal in signals:
                column = lax.optimization_barrier(jnp.sum(signal * refined, axis=2))
                acc = acc + signal * (maskf * noise_weight * column * scale_q * scale_q)[:, :, None]
            return v + transpose_refine(acc, kernel) / SAMPLES
        step = jnp.zeros_like(latent)
        residual = -gradient
        direction = residual
        norm_now = jnp.sum(residual * residual)
        for inner in range(ITERS):
            image = metric(direction)
            alpha = norm_now / jnp.sum(direction * image)
            step = step + alpha * direction
            residual = residual - alpha * image
            norm_next = jnp.sum(residual * residual)
            direction = residual + norm_next / norm_now * direction
            norm_now = norm_next
        latent = latent + step
    return (latent, residual)
```

```python
import functools

import jax
import jax.numpy as jnp
from jax import lax
from jax.experimental import pallas as pl
from jax.experimental.pallas import tpu as pltpu
from jax.sharding import Mesh, PartitionSpec as P

NEWTON = 2
ITERS = 3
PAIRS = 4
SAMPLES = 8
ROWS = 24
SHRINK = 2.0**-10
VMEM = 48 * 1024 * 1024


def shift_up(v, first):
    return jnp.where(first, 0.0, pltpu.roll(v, 1, 0))


def shift_down(v, last):
    return jnp.where(last, 0.0, pltpu.roll(v, v.shape[0] - 1, 0))


def edges(shape):
    row = lax.broadcasted_iota(jnp.int32, shape, 0)
    return row == 0, row == shape[0] - 1


def refine(v, taps, ends):
    even, odd = v
    return (
        taps[0] * shift_up(odd, ends[0]) + taps[1] * even + taps[2] * odd,
        taps[0] * even + taps[1] * odd + taps[2] * shift_down(even, ends[1]),
    )


def transpose_refine(u, taps, ends):
    even, odd = u
    return (
        taps[0] * odd + taps[1] * even + taps[2] * shift_up(odd, ends[0]),
        taps[0] * shift_down(even, ends[1]) + taps[1] * odd + taps[2] * even,
    )


def wide(column):
    return jnp.concatenate([column, column], axis=1)


def back(base, field, factors, weight, offset, taps, ends, scale):
    terms = []
    for p in range(2):
        w = base[p] if field is None else base[p] * field[p]
        total = None
        for k in range(SAMPLES):
            factor = factors[k, p]
            column = weight[p] * jnp.sum(factor * w, axis=1, keepdims=True)
            if offset is not None:
                column = column - offset[p]
            term = factor * wide(column)
            total = term if total is None else total + term
        terms.append(base[p] * total)
    return tuple(scale * t for t in transpose_refine(terms, taps, ends))


def dot(a, b):
    total = a[0] * b[0] + a[1] * b[1]
    total = jnp.sum(total[:, :128] + total[:, 128:], axis=0, keepdims=True)
    return jnp.sum(total, axis=1, keepdims=True)


def moments_row(basis):
    pairs = [(0, 0), (0, 1), (1, 1), (1, 2), (2, 2), (2, 3)]
    lane = lax.broadcasted_iota(jnp.int32, (1, 128), 1)
    row = jnp.zeros((1, 128), jnp.float32)
    for n, (i, j) in enumerate(pairs):
        row = jnp.where(lane == n, dot(basis[i], basis[j]), row)
    return row


def coefficients(row):
    lane = lax.broadcasted_iota(jnp.int32, (1, 128), 1)
    nu = [jnp.sum(jnp.where(lane == n, row, 0.0), axis=1, keepdims=True) for n in range(2 * ITERS)]
    zero, one = jnp.zeros((1, 1), jnp.float32), jnp.ones((1, 1), jnp.float32)

    def inner(a, b):
        total = zero
        for i, x in enumerate(a):
            for j, y in enumerate(b):
                if i + j < 2 * ITERS:
                    total = total + x * y * nu[i + j]
        return total

    def ratio(a, b):
        return jnp.where(b > 0.0, a / jnp.where(b > 0.0, b, 1.0), 0.0)

    residual = [one]
    direction = [one]
    step = [zero] * ITERS
    norm_now = nu[0]
    for it in range(ITERS):
        padded = direction + [zero]
        image = [padded[0]] + [padded[j] + (1.0 / SHRINK) * padded[j - 1] for j in range(1, len(padded))]
        alpha = ratio(norm_now, inner(direction, image))
        step = [s + alpha * direction[j] if j < len(direction) else s for j, s in enumerate(step)]
        residual = [r - alpha * i for r, i in zip(residual + [zero], image)]
        if it < ITERS - 1:
            norm_next = inner(residual, residual)
            beta = ratio(norm_next, norm_now)
            direction = [r + beta * d for r, d in zip(residual, direction + [zero])]
            norm_now = norm_next
    return step, residual


def combine(coefs, basis):
    out = []
    for p in range(2):
        total = coefs[0] * basis[0][p]
        for c, b in zip(coefs[1:], basis[1:]):
            total = total + c * b[p]
        out.append(total)
    return tuple(out)


def krylov(latent, factors, weight, offset, taps, ends):
    base = tuple(jnp.exp(t) for t in refine(latent, taps, ends))
    pulled = back(base, None, factors, weight, offset, taps, ends, 1.0 / SAMPLES)
    basis = [tuple(-m - t for m, t in zip(latent, pulled))]
    for _ in range(ITERS):
        basis.append(
            back(base, refine(basis[-1], taps, ends), factors, weight, None, taps, ends, SHRINK / SAMPLES)
        )
    return basis


def pack_kernel(member, mean, draws, mask, noise, data, out, block, *, count, copies, lines):
    first = member[0] * count
    for a in range(1 + PAIRS):
        for p in range(2):
            for h in range(2):
                lanes = slice(h * 128, h * 128 + 128)
                rows = mean[p, :, lanes] if a == 0 else draws[a - 1, p, :, lanes]
                block[pl.ds(a * 4 + p * 2 + h, count, stride=ROWS), :] = rows
    row = lax.broadcasted_iota(jnp.int32, (count, 128), 0)
    lane = lax.broadcasted_iota(jnp.int32, (count, 128), 1)
    mine = lane == row + first
    noisy = mask[...].astype(jnp.float32) * noise[...]
    for n, values in enumerate((noisy * (1.0 / 256.0), noisy * data[...])):
        for p in range(2):
            picked = jnp.sum(jnp.where(mine, values[p : p + 1, :], 0.0), axis=1, keepdims=True)
            block[pl.ds(20 + n * 2 + p, count, stride=ROWS), :] = jnp.broadcast_to(picked, (count, 128))
    chunk = lines * ROWS
    for fy in range(count // lines):
        for c in range(copies):
            out[pl.ds((fy * copies + c) * chunk, chunk), :] = block[pl.ds(fy * chunk, chunk), :]


def plane_rows(ref, a, p, n):
    return jnp.concatenate([ref[pl.ds(a * 4 + p * 2 + h, n, stride=ROWS), :] for h in range(2)], axis=1)


def columns(ref, n):
    weight = [ref[pl.ds(20 + p, n, stride=ROWS), :] for p in range(2)]
    offset = [ref[pl.ds(22 + p, n, stride=ROWS), :] for p in range(2)]
    return weight, offset


def first_kernel(packed, kernel, sums, factors, held, *, n):
    taps = [kernel[t : t + 1, :] for t in range(3)]
    ends = edges((n, 256))
    latent = tuple(plane_rows(packed, 0, p, n) for p in range(2))
    for k in range(PAIRS):
        spread = refine(tuple(plane_rows(packed, 1 + k, p, n) for p in range(2)), taps, ends)
        for p in range(2):
            factors[2 * k, p] = jnp.exp(spread[p])
            factors[2 * k + 1, p] = jnp.exp(-spread[p])
    weight, offset = columns(packed, n)
    basis = krylov(latent, factors, weight, offset, taps, ends)
    for p in range(2):
        held[0, p] = latent[p]
        for j in range(ITERS):
            held[1 + j, p] = basis[j][p]
    sums[...] = jnp.broadcast_to(moments_row(basis), sums.shape)


def second_kernel(place, sums, packed, kernel, factors, held, out, block, *, n, groups, lines):
    taps = [kernel[t : t + 1, :] for t in range(3)]
    ends = edges((n, 256))
    step, _ = coefficients(jnp.sum(sums[...], axis=0, keepdims=True))
    basis = [tuple(held[j, p] for p in range(2)) for j in range(1 + ITERS)]
    latent = combine([jnp.ones((1, 1), jnp.float32)] + step, basis)
    weight, offset = columns(packed, n)
    basis = krylov(latent, factors, weight, offset, taps, ends)
    for a, v in enumerate([latent] + basis):
        for p in range(2):
            for h in range(2):
                block[pl.ds(a * 4 + p * 2 + h, n, stride=ROWS), :] = v[p][:, h * 128 : h * 128 + 128]
    chunk = lines * ROWS
    for fy in range(groups):
        start = pl.multiple_of(fy * (n // groups) * ROWS + place[0] * chunk, 8)
        out[pl.ds(fy * chunk, chunk), :] = block[pl.ds(start, chunk), :]
    row = jnp.broadcast_to(moments_row(basis), (groups * lines, 128))
    for r in range(20, ROWS):
        out[pl.ds(r, groups * lines, stride=ROWS), :] = row


def last_kernel(gathered, mean_final, cg_residual, *, order, count):
    n = len(order) * count
    step, residual = coefficients(jnp.sum(gathered[pl.ds(20, n, stride=ROWS), :], axis=0, keepdims=True))
    for q, member in enumerate(order):
        for p in range(2):
            for h in range(2):
                v = [
                    gathered[pl.ds(q * count * ROWS + a * 4 + p * 2 + h, count, stride=ROWS), :]
                    for a in range(2 + ITERS)
                ]
                latent = v[0]
                for c, b in zip(step, v[1:]):
                    latent = latent + c * b
                rest = residual[0] * v[1]
                for c, b in zip(residual[1:], v[2:]):
                    rest = rest + c * b
                where = (p, slice(member * count, member * count + count), slice(h * 128, h * 128 + 128))
                mean_final[where] = latent
                cg_residual[where] = rest


def local(mean_start, sample_draws, kernel, sight_mask, noise_weight, data):
    nx, nc, nfy, nzq, nzl = (lax.axis_size(a) for a in ("x", "core", "fy", "zq", "zl"))
    members = nx * nc
    fields = nfy * nzq * nzl
    count = mean_start.shape[1] // members
    depth = mean_start.shape[2]
    f32 = functools.partial(jax.ShapeDtypeStruct, dtype=jnp.float32)
    params = pltpu.CompilerParams(vmem_limit_bytes=VMEM)
    whole = pl.BlockSpec(memory_space=pltpu.VMEM)
    member = (lax.axis_index("x") * nc + lax.axis_index("core")).astype(jnp.int32).reshape(1)
    place = lax.axis_index("zq").astype(jnp.int32).reshape(1)

    packed = pl.pallas_call(
        functools.partial(pack_kernel, count=count, copies=nzq, lines=nzl),
        out_shape=f32((fields * ROWS, 128)),
        grid_spec=pltpu.PrefetchScalarGridSpec(
            num_scalar_prefetch=1,
            grid=(1,),
            in_specs=[
                pl.BlockSpec((2, count, depth), lambda i, s: (0, s[0], 0)),
                pl.BlockSpec((PAIRS, 2, count, depth), lambda i, s: (0, 0, s[0], 0)),
                pl.BlockSpec(sight_mask.shape, lambda i, s: (0, 0)),
                pl.BlockSpec(noise_weight.shape, lambda i, s: (0, 0)),
                pl.BlockSpec(data.shape, lambda i, s: (0, 0)),
            ],
            out_specs=pl.BlockSpec((fields * ROWS, 128), lambda i, s: (0, 0)),
            scratch_shapes=[pltpu.VMEM((count * ROWS, 128), jnp.float32)],
        ),
        compiler_params=params,
        name="pack",
    )(member, mean_start, sample_draws, sight_mask, noise_weight, data)

    packed = lax.all_to_all(packed.reshape(fields, ROWS, 128), ("fy", "zq", "zl"), 0, 0, tiled=True)
    packed = packed.reshape(fields * ROWS, 128)

    cube = members * nfy * nzl
    sums, factors, held = pl.pallas_call(
        functools.partial(first_kernel, n=fields),
        out_shape=[
            f32((cube, 128)),
            f32((SAMPLES, 2, fields, depth)),
            f32((1 + ITERS, 2, fields, depth)),
        ],
        in_specs=[whole, whole],
        out_specs=[whole, whole, whole],
        compiler_params=params,
        name="first",
    )(packed, kernel)

    sums = lax.all_to_all(sums.reshape(cube, 1, 128), ("x", "core", "fy", "zl"), 0, 0, tiled=True)
    sums = sums.reshape(cube, 128)

    lines = nfy * nzl
    found = pl.pallas_call(
        functools.partial(second_kernel, n=fields, groups=nfy, lines=nzl),
        out_shape=f32((lines * ROWS, 128)),
        in_specs=[pl.BlockSpec(memory_space=pltpu.SMEM)] + [whole] * 5,
        out_specs=whole,
        scratch_shapes=[pltpu.VMEM((fields * ROWS, 128), jnp.float32)],
        compiler_params=params,
        name="second",
    )(place, sums, packed, kernel, factors, held)

    found = lax.all_to_all(found.reshape(lines, ROWS, 128), ("fy", "zl"), 0, 0, tiled=True)
    found = lax.all_gather(found.reshape(lines * ROWS, 128), "x")
    found = lax.all_gather(found.reshape(nx * lines * ROWS, 128), "core")
    found = found.reshape(members * lines * ROWS, 128)

    order = tuple(x * nc + c for c in range(nc) for x in range(nx))
    return pl.pallas_call(
        functools.partial(last_kernel, order=order, count=count),
        out_shape=[f32(mean_start.shape), f32(mean_start.shape)],
        in_specs=[whole],
        out_specs=[whole, whole],
        compiler_params=params,
        name="last",
    )(found)


def solution(mesh):
    split = Mesh(mesh.devices.reshape(4, 2, 4, 4, 4), ("x", "core", "fy", "zq", "zl"))
    field = ("fy", "zq", "zl")
    placed = (
        P(field, None, None),
        P(None, field, None, None),
        P(),
        P(field, None),
        P(field, None),
        P(field, None),
    )
    return jax.shard_map(
        local,
        mesh=split,
        in_specs=placed,
        out_specs=(P(field, None, None), P(field, None, None)),
        check_vma=False,
    )
```

```python
import functools

import jax
import jax.numpy as jnp
from jax import lax
from jax.experimental import pallas as pl
from jax.experimental.pallas import tpu as pltpu
from jax.sharding import Mesh, PartitionSpec as P

NEWTON = 2
ITERS = 3
PAIRS = 4
SAMPLES = 8
ROWS = 24
SHRINK = 2.0**-10
VMEM = 48 * 1024 * 1024
FULL = 60 * 1024 * 1024


def shift_up(v, first):
    return jnp.where(first, 0.0, pltpu.roll(v, 1, 0))


def shift_down(v, last):
    return jnp.where(last, 0.0, pltpu.roll(v, v.shape[0] - 1, 0))


def edges(shape):
    row = lax.broadcasted_iota(jnp.int32, shape, 0)
    return row == 0, row == shape[0] - 1


def refine(v, taps, ends):
    even, odd = v
    return (
        taps[0] * shift_up(odd, ends[0]) + taps[1] * even + taps[2] * odd,
        taps[0] * even + taps[1] * odd + taps[2] * shift_down(even, ends[1]),
    )


def transpose_refine(u, taps, ends):
    even, odd = u
    return (
        taps[0] * odd + taps[1] * even + taps[2] * shift_up(odd, ends[0]),
        taps[0] * shift_down(even, ends[1]) + taps[1] * odd + taps[2] * even,
    )


def wide(column):
    return jnp.concatenate([column, column], axis=1)


def back(base, field, factors, weight, offset, taps, ends, scale):
    terms = []
    for p in range(2):
        w = base[p] if field is None else base[p] * field[p]
        total = None
        for k in range(SAMPLES):
            factor = factors[k, p]
            column = weight[p] * jnp.sum(factor * w, axis=1, keepdims=True)
            if offset is not None:
                column = column - offset[p]
            term = factor * wide(column)
            total = term if total is None else total + term
        terms.append(base[p] * total)
    return tuple(scale * t for t in transpose_refine(terms, taps, ends))


def dot(a, b):
    total = a[0] * b[0] + a[1] * b[1]
    total = jnp.sum(total[:, :128] + total[:, 128:], axis=0, keepdims=True)
    return jnp.sum(total, axis=1, keepdims=True)


def moments_row(basis):
    pairs = [(0, 0), (0, 1), (1, 1), (1, 2), (2, 2), (2, 3)]
    lane = lax.broadcasted_iota(jnp.int32, (1, 128), 1)
    row = jnp.zeros((1, 128), jnp.float32)
    for n, (i, j) in enumerate(pairs):
        row = jnp.where(lane == n, dot(basis[i], basis[j]), row)
    return row


def coefficients(row):
    lane = lax.broadcasted_iota(jnp.int32, (1, 128), 1)
    nu = [jnp.sum(jnp.where(lane == n, row, 0.0), axis=1, keepdims=True) for n in range(2 * ITERS)]
    zero, one = jnp.zeros((1, 1), jnp.float32), jnp.ones((1, 1), jnp.float32)

    def inner(a, b):
        total = zero
        for i, x in enumerate(a):
            for j, y in enumerate(b):
                if i + j < 2 * ITERS:
                    total = total + x * y * nu[i + j]
        return total

    def ratio(a, b):
        return jnp.where(b > 0.0, a / jnp.where(b > 0.0, b, 1.0), 0.0)

    residual = [one]
    direction = [one]
    step = [zero] * ITERS
    norm_now = nu[0]
    for it in range(ITERS):
        padded = direction + [zero]
        image = [padded[0]] + [padded[j] + (1.0 / SHRINK) * padded[j - 1] for j in range(1, len(padded))]
        alpha = ratio(norm_now, inner(direction, image))
        step = [s + alpha * direction[j] if j < len(direction) else s for j, s in enumerate(step)]
        residual = [r - alpha * i for r, i in zip(residual + [zero], image)]
        if it < ITERS - 1:
            norm_next = inner(residual, residual)
            beta = ratio(norm_next, norm_now)
            direction = [r + beta * d for r, d in zip(residual, direction + [zero])]
            norm_now = norm_next
    return step, residual


def combine(coefs, basis):
    out = []
    for p in range(2):
        total = coefs[0] * basis[0][p]
        for c, b in zip(coefs[1:], basis[1:]):
            total = total + c * b[p]
        out.append(total)
    return tuple(out)


def krylov(latent, factors, weight, offset, taps, ends):
    base = tuple(jnp.exp(t) for t in refine(latent, taps, ends))
    pulled = back(base, None, factors, weight, offset, taps, ends, 1.0 / SAMPLES)
    basis = [tuple(-m - t for m, t in zip(latent, pulled))]
    for _ in range(ITERS):
        basis.append(
            back(base, refine(basis[-1], taps, ends), factors, weight, None, taps, ends, SHRINK / SAMPLES)
        )
    return basis


def pack_kernel(
    member, mean_all, draws_all, mask_all, noise_all, data_all, out,
    mean, draws, mask, noise, data, block, sems, *, count, copies, lines,
):
    first = pl.multiple_of(member[0] * count, count)
    mine = pl.ds(first, count)
    loads = [
        pltpu.make_async_copy(source, target, sems.at[n])
        for n, (source, target) in enumerate(
            [
                (mean_all.at[:, mine, :], mean),
                (draws_all.at[:, :, mine, :], draws),
                (mask_all, mask),
                (noise_all, noise),
                (data_all, data),
            ]
        )
    ]
    for load in loads:
        load.start()
    for load in loads:
        load.wait()
    for a in range(1 + PAIRS):
        for p in range(2):
            for h in range(2):
                lanes = slice(h * 128, h * 128 + 128)
                rows = mean[p, :, lanes] if a == 0 else draws[a - 1, p, :, lanes]
                block[pl.ds(a * 4 + p * 2 + h, count, stride=ROWS), :] = rows
    row = lax.broadcasted_iota(jnp.int32, (count, 128), 0)
    lane = lax.broadcasted_iota(jnp.int32, (count, 128), 1)
    chosen = lane == row + first
    noisy = mask[...].astype(jnp.float32) * noise[...]
    for n, values in enumerate((noisy * (1.0 / 256.0), noisy * data[...])):
        for p in range(2):
            picked = jnp.sum(jnp.where(chosen, values[p : p + 1, :], 0.0), axis=1, keepdims=True)
            block[pl.ds(20 + n * 2 + p, count, stride=ROWS), :] = jnp.broadcast_to(picked, (count, 128))
    chunk = lines * ROWS
    for fy in range(count // lines):
        for c in range(copies):
            out[pl.ds((fy * copies + c) * chunk, chunk), :] = block[pl.ds(fy * chunk, chunk), :]


def plane_rows(ref, a, p, n):
    return jnp.concatenate([ref[pl.ds(a * 4 + p * 2 + h, n, stride=ROWS), :] for h in range(2)], axis=1)


def columns(ref, n):
    weight = [ref[pl.ds(20 + p, n, stride=ROWS), :] for p in range(2)]
    offset = [ref[pl.ds(22 + p, n, stride=ROWS), :] for p in range(2)]
    return weight, offset


def first_kernel(packed, kernel, sums, factors, held, *, n):
    taps = [kernel[t : t + 1, :] for t in range(3)]
    ends = edges((n, 256))
    latent = tuple(plane_rows(packed, 0, p, n) for p in range(2))
    for k in range(PAIRS):
        spread = refine(tuple(plane_rows(packed, 1 + k, p, n) for p in range(2)), taps, ends)
        for p in range(2):
            factors[2 * k, p] = jnp.exp(spread[p])
            factors[2 * k + 1, p] = jnp.exp(-spread[p])
    weight, offset = columns(packed, n)
    basis = krylov(latent, factors, weight, offset, taps, ends)
    for p in range(2):
        held[0, p] = latent[p]
        for j in range(ITERS):
            held[1 + j, p] = basis[j][p]
    sums[...] = jnp.broadcast_to(moments_row(basis), sums.shape)


def second_kernel(place, sums, packed, kernel, factors, held, out, block, *, n, groups, lines):
    taps = [kernel[t : t + 1, :] for t in range(3)]
    ends = edges((n, 256))
    step, _ = coefficients(jnp.sum(sums[...], axis=0, keepdims=True))
    basis = [tuple(held[j, p] for p in range(2)) for j in range(1 + ITERS)]
    latent = combine([jnp.ones((1, 1), jnp.float32)] + step, basis)
    weight, offset = columns(packed, n)
    basis = krylov(latent, factors, weight, offset, taps, ends)
    for a, v in enumerate([latent] + basis):
        for p in range(2):
            for h in range(2):
                block[pl.ds(a * 4 + p * 2 + h, n, stride=ROWS), :] = v[p][:, h * 128 : h * 128 + 128]
    chunk = lines * ROWS
    for fy in range(groups):
        start = pl.multiple_of(fy * (n // groups) * ROWS + place[0] * chunk, 8)
        out[pl.ds(fy * chunk, chunk), :] = block[pl.ds(start, chunk), :]
    row = jnp.broadcast_to(moments_row(basis), (groups * lines, 128))
    for r in range(20, ROWS):
        out[pl.ds(r, groups * lines, stride=ROWS), :] = row


def last_kernel(core, found, other, mean_final, cg_residual, *, chips, count):
    n = chips * count
    sums = found[pl.ds(20, n, stride=ROWS), :] + other[pl.ds(20, n, stride=ROWS), :]
    step, residual = coefficients(jnp.sum(sums, axis=0, keepdims=True))
    for ref, owner in ((found, core[0]), (other, 1 - core[0])):
        for x in range(chips):
            rows = pl.ds(pl.multiple_of((2 * x + owner) * count, count), count)
            for p in range(2):
                for h in range(2):
                    v = [
                        ref[pl.ds(x * count * ROWS + a * 4 + p * 2 + h, count, stride=ROWS), :]
                        for a in range(2 + ITERS)
                    ]
                    latent = v[0]
                    for c, b in zip(step, v[1:]):
                        latent = latent + c * b
                    rest = residual[0] * v[1]
                    for c, b in zip(residual[1:], v[2:]):
                        rest = rest + c * b
                    mean_final[p, rows, h * 128 : h * 128 + 128] = latent
                    cg_residual[p, rows, h * 128 : h * 128 + 128] = rest


def local(mean_start, sample_draws, kernel, sight_mask, noise_weight, data):
    nx, nc, nfy, nzq, nzl = (lax.axis_size(a) for a in ("x", "core", "fy", "zq", "zl"))
    members = nx * nc
    fields = nfy * nzq * nzl
    count = mean_start.shape[1] // members
    depth = mean_start.shape[2]
    f32 = functools.partial(jax.ShapeDtypeStruct, dtype=jnp.float32)
    params = pltpu.CompilerParams(vmem_limit_bytes=VMEM)
    whole = pl.BlockSpec(memory_space=pltpu.VMEM)
    member = (lax.axis_index("x") * nc + lax.axis_index("core")).astype(jnp.int32).reshape(1)
    place = lax.axis_index("zq").astype(jnp.int32).reshape(1)

    packed = pl.pallas_call(
        functools.partial(pack_kernel, count=count, copies=nzq, lines=nzl),
        out_shape=f32((fields * ROWS, 128)),
        in_specs=[pl.BlockSpec(memory_space=pltpu.SMEM)] + [pl.BlockSpec(memory_space=pltpu.HBM)] * 5,
        out_specs=whole,
        scratch_shapes=[
            pltpu.VMEM((2, count, depth), jnp.float32),
            pltpu.VMEM((PAIRS, 2, count, depth), jnp.float32),
            pltpu.VMEM(sight_mask.shape, jnp.int32),
            pltpu.VMEM(noise_weight.shape, jnp.float32),
            pltpu.VMEM(data.shape, jnp.float32),
            pltpu.VMEM((count * ROWS, 128), jnp.float32),
            pltpu.SemaphoreType.DMA((5,)),
        ],
        compiler_params=pltpu.CompilerParams(vmem_limit_bytes=FULL),
        name="pack",
    )(member, mean_start, sample_draws, sight_mask, noise_weight, data)

    packed = lax.all_to_all(packed.reshape(fields, ROWS, 128), ("fy", "zq", "zl"), 0, 0, tiled=True)
    packed = packed.reshape(fields * ROWS, 128)

    cube = members * nfy * nzl
    sums, factors, held = pl.pallas_call(
        functools.partial(first_kernel, n=fields),
        out_shape=[
            f32((cube, 128)),
            f32((SAMPLES, 2, fields, depth)),
            f32((1 + ITERS, 2, fields, depth)),
        ],
        in_specs=[whole, whole],
        out_specs=[whole, whole, whole],
        compiler_params=params,
        name="first",
    )(packed, kernel)

    sums = lax.all_to_all(sums.reshape(cube, 1, 128), ("x", "core", "fy", "zl"), 0, 0, tiled=True)
    sums = sums.reshape(cube, 128)

    lines = nfy * nzl
    found = pl.pallas_call(
        functools.partial(second_kernel, n=fields, groups=nfy, lines=nzl),
        out_shape=f32((lines * ROWS, 128)),
        in_specs=[pl.BlockSpec(memory_space=pltpu.SMEM)] + [whole] * 5,
        out_specs=whole,
        scratch_shapes=[pltpu.VMEM((fields * ROWS, 128), jnp.float32)],
        compiler_params=params,
        name="second",
    )(place, sums, packed, kernel, factors, held)

    found = lax.all_to_all(found.reshape(lines, ROWS, 128), ("fy", "zl"), 0, 0, tiled=True)
    found = lax.all_gather(found.reshape(lines * ROWS, 128), "x")
    found = found.reshape(nx * lines * ROWS, 128)
    other = lax.ppermute(found, "core", [(0, 1), (1, 0)])
    core = lax.axis_index("core").astype(jnp.int32).reshape(1)
    return pl.pallas_call(
        functools.partial(last_kernel, chips=nx, count=count),
        out_shape=[f32(mean_start.shape), f32(mean_start.shape)],
        in_specs=[pl.BlockSpec(memory_space=pltpu.SMEM), whole, whole],
        out_specs=[whole, whole],
        compiler_params=params,
        name="last",
    )(core, found, other)


def solution(mesh):
    split = Mesh(mesh.devices.reshape(4, 2, 4, 4, 4), ("x", "core", "fy", "zq", "zl"))
    field = ("fy", "zq", "zl")
    placed = (
        P(field, None, None),
        P(None, field, None, None),
        P(),
        P(field, None),
        P(field, None),
        P(field, None),
    )
    return jax.shard_map(
        local,
        mesh=split,
        in_specs=placed,
        out_specs=(P(field, None, None), P(field, None, None)),
        check_vma=False,
    )
```

```python
import functools

import jax
import jax.numpy as jnp
from jax import lax
from jax.experimental import pallas as pl
from jax.experimental.pallas import tpu as pltpu
from jax.sharding import Mesh, PartitionSpec as P

NEWTON = 2
ITERS = 3
PAIRS = 4
SAMPLES = 8
ROWS = 24
SHRINK = 2.0**-10
VMEM = 48 * 1024 * 1024
FULL = 60 * 1024 * 1024


def shift_up(v, first):
    return jnp.where(first, 0.0, pltpu.roll(v, 1, 0))


def shift_down(v, last):
    return jnp.where(last, 0.0, pltpu.roll(v, v.shape[0] - 1, 0))


def edges(shape):
    row = lax.broadcasted_iota(jnp.int32, shape, 0)
    return row == 0, row == shape[0] - 1


def refine(v, taps, ends):
    even, odd = v
    return (
        taps[0] * shift_up(odd, ends[0]) + taps[1] * even + taps[2] * odd,
        taps[0] * even + taps[1] * odd + taps[2] * shift_down(even, ends[1]),
    )


def transpose_refine(u, taps, ends):
    even, odd = u
    return (
        taps[0] * odd + taps[1] * even + taps[2] * shift_up(odd, ends[0]),
        taps[0] * shift_down(even, ends[1]) + taps[1] * odd + taps[2] * even,
    )


def wide(column):
    return jnp.concatenate([column, column], axis=1)


def back(base, field, factors, weight, offset, taps, ends, scale):
    terms = []
    for p in range(2):
        w = base[p] if field is None else base[p] * field[p]
        total = None
        for k in range(SAMPLES):
            factor = factors[k, p]
            column = weight[p] * jnp.sum(factor * w, axis=1, keepdims=True)
            if offset is not None:
                column = column - offset[p]
            term = factor * wide(column)
            total = term if total is None else total + term
        terms.append(base[p] * total)
    return tuple(scale * t for t in transpose_refine(terms, taps, ends))


def dot(a, b):
    total = a[0] * b[0] + a[1] * b[1]
    total = jnp.sum(total[:, :128] + total[:, 128:], axis=0, keepdims=True)
    return jnp.sum(total, axis=1, keepdims=True)


def moments_row(basis):
    pairs = [(0, 0), (0, 1), (1, 1), (1, 2), (2, 2), (2, 3)]
    lane = lax.broadcasted_iota(jnp.int32, (1, 128), 1)
    row = jnp.zeros((1, 128), jnp.float32)
    for n, (i, j) in enumerate(pairs):
        row = jnp.where(lane == n, dot(basis[i], basis[j]), row)
    return row


def coefficients(row):
    lane = lax.broadcasted_iota(jnp.int32, (1, 128), 1)
    nu = [jnp.sum(jnp.where(lane == n, row, 0.0), axis=1, keepdims=True) for n in range(2 * ITERS)]
    zero, one = jnp.zeros((1, 1), jnp.float32), jnp.ones((1, 1), jnp.float32)

    def inner(a, b):
        total = zero
        for i, x in enumerate(a):
            for j, y in enumerate(b):
                if i + j < 2 * ITERS:
                    total = total + x * y * nu[i + j]
        return total

    def ratio(a, b):
        return jnp.where(b > 0.0, a / jnp.where(b > 0.0, b, 1.0), 0.0)

    residual = [one]
    direction = [one]
    step = [zero] * ITERS
    norm_now = nu[0]
    for it in range(ITERS):
        padded = direction + [zero]
        image = [padded[0]] + [padded[j] + (1.0 / SHRINK) * padded[j - 1] for j in range(1, len(padded))]
        alpha = ratio(norm_now, inner(direction, image))
        step = [s + alpha * direction[j] if j < len(direction) else s for j, s in enumerate(step)]
        residual = [r - alpha * i for r, i in zip(residual + [zero], image)]
        if it < ITERS - 1:
            norm_next = inner(residual, residual)
            beta = ratio(norm_next, norm_now)
            direction = [r + beta * d for r, d in zip(residual, direction + [zero])]
            norm_now = norm_next
    return step, residual


def combine(coefs, basis):
    out = []
    for p in range(2):
        total = coefs[0] * basis[0][p]
        for c, b in zip(coefs[1:], basis[1:]):
            total = total + c * b[p]
        out.append(total)
    return tuple(out)


def krylov(latent, factors, weight, offset, taps, ends):
    base = tuple(jnp.exp(t) for t in refine(latent, taps, ends))
    pulled = back(base, None, factors, weight, offset, taps, ends, 1.0 / SAMPLES)
    basis = [tuple(-m - t for m, t in zip(latent, pulled))]
    for _ in range(ITERS):
        basis.append(
            back(base, refine(basis[-1], taps, ends), factors, weight, None, taps, ends, SHRINK / SAMPLES)
        )
    return basis


def pack_kernel(
    member, mean_all, draws_all, mask_all, noise_all, data_all, out,
    mean, draws, mask, noise, data, sems, *, count,
):
    first = pl.multiple_of(member[0] * count, count)
    mine = pl.ds(first, count)
    loads = [
        pltpu.make_async_copy(source, target, sems.at[n])
        for n, (source, target) in enumerate(
            [
                (mean_all.at[:, mine, :], mean),
                (draws_all.at[:, :, mine, :], draws),
                (mask_all, mask),
                (noise_all, noise),
                (data_all, data),
            ]
        )
    ]
    for load in loads:
        load.start()
    for load in loads:
        load.wait()
    for a in range(1 + PAIRS):
        for p in range(2):
            for h in range(2):
                lanes = slice(h * 128, h * 128 + 128)
                rows = mean[p, :, lanes] if a == 0 else draws[a - 1, p, :, lanes]
                out[pl.ds(a * 4 + p * 2 + h, count, stride=ROWS), :] = rows
    row = lax.broadcasted_iota(jnp.int32, (count, 128), 0)
    lane = lax.broadcasted_iota(jnp.int32, (count, 128), 1)
    chosen = lane == row + first
    noisy = mask[...].astype(jnp.float32) * noise[...]
    for n, values in enumerate((noisy * (1.0 / 256.0), noisy * data[...])):
        for p in range(2):
            picked = jnp.sum(jnp.where(chosen, values[p : p + 1, :], 0.0), axis=1, keepdims=True)
            out[pl.ds(20 + n * 2 + p, count, stride=ROWS), :] = jnp.broadcast_to(picked, (count, 128))


def plane_rows(ref, a, p, n):
    return jnp.concatenate([ref[pl.ds(a * 4 + p * 2 + h, n, stride=ROWS), :] for h in range(2)], axis=1)


def columns(ref, n):
    weight = [ref[pl.ds(20 + p, n, stride=ROWS), :] for p in range(2)]
    offset = [ref[pl.ds(22 + p, n, stride=ROWS), :] for p in range(2)]
    return weight, offset


def first_kernel(packed, kernel, sums, factors, held, *, n):
    taps = [kernel[t : t + 1, :] for t in range(3)]
    ends = edges((n, 256))
    latent = tuple(plane_rows(packed, 0, p, n) for p in range(2))
    for k in range(PAIRS):
        spread = refine(tuple(plane_rows(packed, 1 + k, p, n) for p in range(2)), taps, ends)
        for p in range(2):
            factors[2 * k, p] = jnp.exp(spread[p])
            factors[2 * k + 1, p] = jnp.exp(-spread[p])
    weight, offset = columns(packed, n)
    basis = krylov(latent, factors, weight, offset, taps, ends)
    for p in range(2):
        held[0, p] = latent[p]
        for j in range(ITERS):
            held[1 + j, p] = basis[j][p]
    sums[...] = jnp.broadcast_to(moments_row(basis), sums.shape)


def second_kernel(place, sums, packed, kernel, factors, held, out, block, *, n, lines):
    taps = [kernel[t : t + 1, :] for t in range(3)]
    ends = edges((n, 256))
    step, _ = coefficients(jnp.sum(sums[...], axis=0, keepdims=True))
    basis = [tuple(held[j, p] for p in range(2)) for j in range(1 + ITERS)]
    latent = combine([jnp.ones((1, 1), jnp.float32)] + step, basis)
    weight, offset = columns(packed, n)
    basis = krylov(latent, factors, weight, offset, taps, ends)
    for a, v in enumerate([latent] + basis):
        for p in range(2):
            for h in range(2):
                block[pl.ds(a * 4 + p * 2 + h, n, stride=ROWS), :] = v[p][:, h * 128 : h * 128 + 128]
    chunk = lines * ROWS
    out[...] = block[pl.ds(pl.multiple_of(place[0] * chunk, 8), chunk), :]
    row = jnp.broadcast_to(moments_row(basis), (lines, 128))
    for r in range(20, ROWS):
        out[pl.ds(r, lines, stride=ROWS), :] = row


def last_kernel(core, found, other, mean_final, cg_residual, *, chips, count):
    n = chips * count
    sums = found[pl.ds(20, n, stride=ROWS), :] + other[pl.ds(20, n, stride=ROWS), :]
    step, residual = coefficients(jnp.sum(sums, axis=0, keepdims=True))
    for ref, owner in ((found, core[0]), (other, 1 - core[0])):
        for x in range(chips):
            rows = pl.ds(pl.multiple_of((2 * x + owner) * count, count), count)
            for p in range(2):
                for h in range(2):
                    v = [
                        ref[pl.ds(x * count * ROWS + a * 4 + p * 2 + h, count, stride=ROWS), :]
                        for a in range(2 + ITERS)
                    ]
                    latent = v[0]
                    for c, b in zip(step, v[1:]):
                        latent = latent + c * b
                    rest = residual[0] * v[1]
                    for c, b in zip(residual[1:], v[2:]):
                        rest = rest + c * b
                    mean_final[p, rows, h * 128 : h * 128 + 128] = latent
                    cg_residual[p, rows, h * 128 : h * 128 + 128] = rest


def spread(block, axis):
    copies = lax.axis_size(axis)
    block = jnp.broadcast_to(block[None], (copies,) + block.shape)
    return lax.all_to_all(block, axis, 0, 0, tiled=True)


def local(mean_start, sample_draws, kernel, sight_mask, noise_weight, data):
    nx, nc, nfy, nfz = (lax.axis_size(a) for a in ("x", "core", "fy", "fz"))
    members = nx * nc
    fields = nfy * nfz
    count = mean_start.shape[1] // members
    depth = mean_start.shape[2]
    f32 = functools.partial(jax.ShapeDtypeStruct, dtype=jnp.float32)
    params = pltpu.CompilerParams(vmem_limit_bytes=VMEM)
    whole = pl.BlockSpec(memory_space=pltpu.VMEM)
    scalar = pl.BlockSpec(memory_space=pltpu.SMEM)
    core = lax.axis_index("core").astype(jnp.int32)
    member = (lax.axis_index("x").astype(jnp.int32) * nc + core).reshape(1)
    place = lax.axis_index("fy").astype(jnp.int32).reshape(1)

    packed = pl.pallas_call(
        functools.partial(pack_kernel, count=count),
        out_shape=f32((nfz * ROWS, 128)),
        in_specs=[scalar] + [pl.BlockSpec(memory_space=pltpu.HBM)] * 5,
        out_specs=whole,
        scratch_shapes=[
            pltpu.VMEM((2, count, depth), jnp.float32),
            pltpu.VMEM((PAIRS, 2, count, depth), jnp.float32),
            pltpu.VMEM(sight_mask.shape, jnp.int32),
            pltpu.VMEM(noise_weight.shape, jnp.float32),
            pltpu.VMEM(data.shape, jnp.float32),
            pltpu.SemaphoreType.DMA((5,)),
        ],
        compiler_params=pltpu.CompilerParams(vmem_limit_bytes=FULL),
        name="pack",
    )(member, mean_start, sample_draws, sight_mask, noise_weight, data)

    packed = lax.all_to_all(packed.reshape(nfz, ROWS, 128), "fz", 0, 0, tiled=True)
    packed = spread(packed.reshape(nfz * ROWS, 128), "fy").reshape(fields * ROWS, 128)

    sharers = members * nfz
    sums, factors, held = pl.pallas_call(
        functools.partial(first_kernel, n=fields),
        out_shape=[
            f32((sharers, 128)),
            f32((SAMPLES, 2, fields, depth)),
            f32((1 + ITERS, 2, fields, depth)),
        ],
        in_specs=[whole, whole],
        out_specs=[whole, whole, whole],
        compiler_params=params,
        name="first",
    )(packed, kernel)

    sums = lax.all_to_all(sums.reshape(sharers, 1, 128), ("x", "core", "fz"), 0, 0, tiled=True)
    sums = sums.reshape(sharers, 128)

    found = pl.pallas_call(
        functools.partial(second_kernel, n=fields, lines=nfz),
        out_shape=f32((nfz * ROWS, 128)),
        in_specs=[scalar] + [whole] * 5,
        out_specs=whole,
        scratch_shapes=[pltpu.VMEM((fields * ROWS, 128), jnp.float32)],
        compiler_params=params,
        name="second",
    )(place, sums, packed, kernel, factors, held)

    found = lax.all_to_all(found.reshape(nfz, ROWS, 128), "fz", 0, 0, tiled=True)
    found = spread(found.reshape(nfz * ROWS, 128), "x").reshape(nx * nfz * ROWS, 128)
    other = lax.ppermute(found, "core", [(0, 1), (1, 0)])

    return pl.pallas_call(
        functools.partial(last_kernel, chips=nx, count=count),
        out_shape=[f32(mean_start.shape), f32(mean_start.shape)],
        in_specs=[scalar, whole, whole],
        out_specs=[whole, whole],
        compiler_params=params,
        name="last",
    )(core.reshape(1), found, other)


def solution(mesh):
    split = Mesh(mesh.devices.reshape(4, 2, 4, 16), ("x", "core", "fy", "fz"))
    field = ("fy", "fz")
    placed = (
        P(field, None, None),
        P(None, field, None, None),
        P(),
        P(field, None),
        P(field, None),
        P(field, None),
    )
    return jax.shard_map(
        local,
        mesh=split,
        in_specs=placed,
        out_specs=(P(field, None, None), P(field, None, None)),
        check_vma=False,
    )
```

```python
import functools

import jax
import jax.numpy as jnp
from jax import lax
from jax.experimental import pallas as pl
from jax.experimental.pallas import tpu as pltpu
from jax.sharding import Mesh, PartitionSpec as P

NEWTON = 2
ITERS = 3
PAIRS = 4
SAMPLES = 8
IN = 21
ROWS = 24
SHRINK = 2.0**-10
VMEM = 48 * 1024 * 1024
FULL = 60 * 1024 * 1024


def shift_up(v, first):
    return jnp.where(first, 0.0, pltpu.roll(v, 1, 0))


def shift_down(v, last):
    return jnp.where(last, 0.0, pltpu.roll(v, v.shape[0] - 1, 0))


def edges(shape):
    row = lax.broadcasted_iota(jnp.int32, shape, 0)
    return row == 0, row == shape[0] - 1


def refine(v, taps, ends):
    even, odd = v
    return (
        taps[0] * shift_up(odd, ends[0]) + taps[1] * even + taps[2] * odd,
        taps[0] * even + taps[1] * odd + taps[2] * shift_down(even, ends[1]),
    )


def transpose_refine(u, taps, ends):
    even, odd = u
    return (
        taps[0] * odd + taps[1] * even + taps[2] * shift_up(odd, ends[0]),
        taps[0] * shift_down(even, ends[1]) + taps[1] * odd + taps[2] * even,
    )


def wide(column):
    return jnp.concatenate([column, column], axis=1)


def back(base, field, factors, weight, offset, taps, ends, scale):
    terms = []
    for p in range(2):
        w = base[p] if field is None else base[p] * field[p]
        total = None
        for k in range(SAMPLES):
            factor = factors[k, p]
            column = weight[p] * jnp.sum(factor * w, axis=1, keepdims=True)
            if offset is not None:
                column = column - offset[p]
            term = factor * wide(column)
            total = term if total is None else total + term
        terms.append(base[p] * total)
    return tuple(scale * t for t in transpose_refine(terms, taps, ends))


def dot(a, b):
    total = a[0] * b[0] + a[1] * b[1]
    total = jnp.sum(total[:, :128] + total[:, 128:], axis=0, keepdims=True)
    return jnp.sum(total, axis=1, keepdims=True)


def moments_row(basis):
    pairs = [(0, 0), (0, 1), (1, 1), (1, 2), (2, 2), (2, 3)]
    lane = lax.broadcasted_iota(jnp.int32, (1, 128), 1)
    row = jnp.zeros((1, 128), jnp.float32)
    for n, (i, j) in enumerate(pairs):
        row = jnp.where(lane == n, dot(basis[i], basis[j]), row)
    return row


def coefficients(row):
    lane = lax.broadcasted_iota(jnp.int32, (1, 128), 1)
    nu = [jnp.sum(jnp.where(lane == n, row, 0.0), axis=1, keepdims=True) for n in range(2 * ITERS)]
    zero, one = jnp.zeros((1, 1), jnp.float32), jnp.ones((1, 1), jnp.float32)

    def inner(a, b):
        total = zero
        for i, x in enumerate(a):
            for j, y in enumerate(b):
                if i + j < 2 * ITERS:
                    total = total + x * y * nu[i + j]
        return total

    def ratio(a, b):
        return jnp.where(b > 0.0, a / jnp.where(b > 0.0, b, 1.0), 0.0)

    residual = [one]
    direction = [one]
    step = [zero] * ITERS
    norm_now = nu[0]
    for it in range(ITERS):
        padded = direction + [zero]
        image = [padded[0]] + [padded[j] + (1.0 / SHRINK) * padded[j - 1] for j in range(1, len(padded))]
        alpha = ratio(norm_now, inner(direction, image))
        step = [s + alpha * direction[j] if j < len(direction) else s for j, s in enumerate(step)]
        residual = [r - alpha * i for r, i in zip(residual + [zero], image)]
        if it < ITERS - 1:
            norm_next = inner(residual, residual)
            beta = ratio(norm_next, norm_now)
            direction = [r + beta * d for r, d in zip(residual, direction + [zero])]
            norm_now = norm_next
    return step, residual


def combine(coefs, basis):
    out = []
    for p in range(2):
        total = coefs[0] * basis[0][p]
        for c, b in zip(coefs[1:], basis[1:]):
            total = total + c * b[p]
        out.append(total)
    return tuple(out)


def krylov(latent, factors, weight, offset, taps, ends):
    base = tuple(jnp.exp(t) for t in refine(latent, taps, ends))
    pulled = back(base, None, factors, weight, offset, taps, ends, 1.0 / SAMPLES)
    basis = [tuple(-m - t for m, t in zip(latent, pulled))]
    for _ in range(ITERS):
        basis.append(
            back(base, refine(basis[-1], taps, ends), factors, weight, None, taps, ends, SHRINK / SAMPLES)
        )
    return basis


def pack_kernel(
    code, mean_all, draws_all, mask_all, noise_all, data_all, out,
    mean, draws, mask, noise, data, sems, *, count, members,
):
    first = pl.multiple_of((code[0] % members) * count, count)
    mine = pl.ds(first, count)
    loads = [
        pltpu.make_async_copy(source, target, sems.at[n])
        for n, (source, target) in enumerate(
            [
                (mean_all.at[:, mine, :], mean),
                (draws_all.at[:, :, mine, :], draws),
                (mask_all, mask),
                (noise_all, noise),
                (data_all, data),
            ]
        )
    ]
    for load in loads:
        load.start()
    for load in loads:
        load.wait()
    for a in range(1 + PAIRS):
        for p in range(2):
            for h in range(2):
                lanes = slice(h * 128, h * 128 + 128)
                rows = mean[p, :, lanes] if a == 0 else draws[a - 1, p, :, lanes]
                out[pl.ds(a * 4 + p * 2 + h, count, stride=IN), :] = rows
    row = lax.broadcasted_iota(jnp.int32, (count, 128), 0)
    lane = lax.broadcasted_iota(jnp.int32, (count, 128), 1)
    chosen = lane == row + first
    noisy = mask[...].astype(jnp.float32) * noise[...]
    extra = jnp.zeros((count, 128), jnp.float32)
    for n, values in enumerate((noisy * (1.0 / 256.0), noisy * data[...])):
        for p in range(2):
            picked = jnp.sum(jnp.where(chosen, values[p : p + 1, :], 0.0), axis=1, keepdims=True)
            extra = jnp.where(lane == n * 2 + p, picked, extra)
    out[pl.ds(20, count, stride=IN), :] = extra


def plane_rows(ref, a, p, n):
    return jnp.concatenate([ref[pl.ds(a * 4 + p * 2 + h, n, stride=IN), :] for h in range(2)], axis=1)


def columns(ref, n):
    extra = ref[pl.ds(20, n, stride=IN), :]
    spread = [jnp.broadcast_to(extra[:, c : c + 1], extra.shape) for c in range(4)]
    return spread[:2], spread[2:]


def first_kernel(packed, kernel, sums, factors, held, *, n):
    taps = [kernel[t : t + 1, :] for t in range(3)]
    ends = edges((n, 256))
    latent = tuple(plane_rows(packed, 0, p, n) for p in range(2))
    for k in range(PAIRS):
        spread = refine(tuple(plane_rows(packed, 1 + k, p, n) for p in range(2)), taps, ends)
        for p in range(2):
            factors[2 * k, p] = jnp.exp(spread[p])
            factors[2 * k + 1, p] = jnp.exp(-spread[p])
    weight, offset = columns(packed, n)
    basis = krylov(latent, factors, weight, offset, taps, ends)
    for p in range(2):
        held[0, p] = latent[p]
        for j in range(ITERS):
            held[1 + j, p] = basis[j][p]
    sums[...] = moments_row(basis)


def second_kernel(code, sums, packed, kernel, factors, held, out, block, *, n, groups, lines, members):
    taps = [kernel[t : t + 1, :] for t in range(3)]
    ends = edges((n, 256))
    step, _ = coefficients(jnp.sum(sums[...], axis=0, keepdims=True))
    basis = [tuple(held[j, p] for p in range(2)) for j in range(1 + ITERS)]
    latent = combine([jnp.ones((1, 1), jnp.float32)] + step, basis)
    weight, offset = columns(packed, n)
    basis = krylov(latent, factors, weight, offset, taps, ends)
    for a, v in enumerate([latent] + basis):
        for p in range(2):
            for h in range(2):
                block[pl.ds(a * 4 + p * 2 + h, n, stride=ROWS), :] = v[p][:, h * 128 : h * 128 + 128]
    chunk = lines * ROWS
    for fy in range(groups):
        start = pl.multiple_of(fy * (n // groups) * ROWS + (code[0] // members) * chunk, 8)
        out[pl.ds(fy * chunk, chunk), :] = block[pl.ds(start, chunk), :]
    row = jnp.broadcast_to(moments_row(basis), (groups * lines, 128))
    for r in range(20, ROWS):
        out[pl.ds(r, groups * lines, stride=ROWS), :] = row


def last_kernel(code, found, other, mean_final, cg_residual, *, chips, count):
    core = code[0] % 2
    n = chips * count
    sums = found[pl.ds(20, n, stride=ROWS), :] + other[pl.ds(20, n, stride=ROWS), :]
    step, residual = coefficients(jnp.sum(sums, axis=0, keepdims=True))
    for ref, owner in ((found, core), (other, 1 - core)):
        for x in range(chips):
            rows = pl.ds(pl.multiple_of((2 * x + owner) * count, count), count)
            for p in range(2):
                for h in range(2):
                    v = [
                        ref[pl.ds(x * count * ROWS + a * 4 + p * 2 + h, count, stride=ROWS), :]
                        for a in range(2 + ITERS)
                    ]
                    latent = v[0]
                    for c, b in zip(step, v[1:]):
                        latent = latent + c * b
                    rest = residual[0] * v[1]
                    for c, b in zip(residual[1:], v[2:]):
                        rest = rest + c * b
                    mean_final[p, rows, h * 128 : h * 128 + 128] = latent
                    cg_residual[p, rows, h * 128 : h * 128 + 128] = rest


def spread(block, axis):
    copies = lax.axis_size(axis)
    block = jnp.broadcast_to(block[None], (copies,) + block.shape)
    return lax.all_to_all(block, axis, 0, 0, tiled=True)


def local(mean_start, sample_draws, kernel, sight_mask, noise_weight, data):
    nx, nc, nfy, nzq, nzl = (lax.axis_size(a) for a in ("x", "core", "fy", "zq", "zl"))
    members = nx * nc
    fields = nfy * nzq * nzl
    lines = nfy * nzl
    count = mean_start.shape[1] // members
    depth = mean_start.shape[2]
    f32 = functools.partial(jax.ShapeDtypeStruct, dtype=jnp.float32)
    params = pltpu.CompilerParams(vmem_limit_bytes=VMEM)
    whole = pl.BlockSpec(memory_space=pltpu.VMEM)
    scalar = pl.BlockSpec(memory_space=pltpu.SMEM)
    code = lax.axis_index("zq") * members + lax.axis_index("x") * nc + lax.axis_index("core")
    code = code.astype(jnp.int32).reshape(1)

    packed = pl.pallas_call(
        functools.partial(pack_kernel, count=count, members=members),
        out_shape=f32((lines * IN, 128)),
        in_specs=[scalar] + [pl.BlockSpec(memory_space=pltpu.HBM)] * 5,
        out_specs=whole,
        scratch_shapes=[
            pltpu.VMEM((2, count, depth), jnp.float32),
            pltpu.VMEM((PAIRS, 2, count, depth), jnp.float32),
            pltpu.VMEM(sight_mask.shape, jnp.int32),
            pltpu.VMEM(noise_weight.shape, jnp.float32),
            pltpu.VMEM(data.shape, jnp.float32),
            pltpu.SemaphoreType.DMA((5,)),
        ],
        compiler_params=pltpu.CompilerParams(vmem_limit_bytes=FULL),
        name="pack",
    )(code, mean_start, sample_draws, sight_mask, noise_weight, data)

    packed = jnp.broadcast_to(packed.reshape(nfy, 1, nzl * IN, 1, 128), (nfy, nzq, nzl * IN, 1, 128))
    packed = lax.all_to_all(packed.reshape(fields * IN, 1, 128), ("fy", "zq", "zl"), 0, 0, tiled=True)
    packed = packed.reshape(fields * IN, 128)

    sharers = members * lines
    sums, factors, held = pl.pallas_call(
        functools.partial(first_kernel, n=fields),
        out_shape=[
            f32((1, 128)),
            f32((SAMPLES, 2, fields, depth)),
            f32((1 + ITERS, 2, fields, depth)),
        ],
        in_specs=[whole, whole],
        out_specs=[whole, whole, whole],
        compiler_params=params,
        name="first",
    )(packed, kernel)

    sums = jnp.broadcast_to(sums[None], (sharers, 1, 128))
    sums = lax.all_to_all(sums, ("fy", "zl", "x", "core"), 0, 0, tiled=True)
    sums = sums.reshape(sharers, 128)

    found = pl.pallas_call(
        functools.partial(second_kernel, n=fields, groups=nfy, lines=nzl, members=members),
        out_shape=f32((lines * ROWS, 128)),
        in_specs=[scalar] + [whole] * 5,
        out_specs=whole,
        scratch_shapes=[pltpu.VMEM((fields * ROWS, 128), jnp.float32)],
        compiler_params=params,
        name="second",
    )(code, sums, packed, kernel, factors, held)

    found = lax.all_to_all(found.reshape(lines, ROWS, 128), ("fy", "zl"), 0, 0, tiled=True)
    found = spread(found.reshape(lines * ROWS, 128), "x").reshape(nx * lines * ROWS, 128)
    other = lax.ppermute(found, "core", [(0, 1), (1, 0)])

    return pl.pallas_call(
        functools.partial(last_kernel, chips=nx, count=count),
        out_shape=[f32(mean_start.shape), f32(mean_start.shape)],
        in_specs=[scalar, whole, whole],
        out_specs=[whole, whole],
        compiler_params=params,
        name="last",
    )(code, found, other)


def solution(mesh):
    split = Mesh(mesh.devices.reshape(4, 2, 4, 4, 4), ("x", "core", "fy", "zq", "zl"))
    field = ("fy", "zq", "zl")
    placed = (
        P(field, None, None),
        P(None, field, None, None),
        P(),
        P(field, None),
        P(field, None),
        P(field, None),
    )
    return jax.shard_map(
        local,
        mesh=split,
        in_specs=placed,
        out_specs=(P(field, None, None), P(field, None, None)),
        check_vma=False,
    )
```

```python
import functools

import jax
import jax.numpy as jnp
from jax import lax
from jax.experimental import pallas as pl
from jax.experimental.pallas import tpu as pltpu
from jax.sharding import Mesh, PartitionSpec as P

NEWTON = 2
ITERS = 3
PAIRS = 4
SAMPLES = 8
ROWS = 21
HELD = 24
SHRINK = 2.0**-10
VMEM = 48 * 1024 * 1024
FULL = 57 * 1024 * 1024


def shift_up(v, first):
    return jnp.where(first, 0.0, pltpu.roll(v, 1, 0))


def shift_down(v, last):
    return jnp.where(last, 0.0, pltpu.roll(v, v.shape[0] - 1, 0))


def edges(shape):
    row = lax.broadcasted_iota(jnp.int32, shape, 0)
    return row == 0, row == shape[0] - 1


def refine(v, taps, ends):
    even, odd = v
    return (
        taps[0] * shift_up(odd, ends[0]) + taps[1] * even + taps[2] * odd,
        taps[0] * even + taps[1] * odd + taps[2] * shift_down(even, ends[1]),
    )


def transpose_refine(u, taps, ends):
    even, odd = u
    return (
        taps[0] * odd + taps[1] * even + taps[2] * shift_up(odd, ends[0]),
        taps[0] * shift_down(even, ends[1]) + taps[1] * odd + taps[2] * even,
    )


def wide(column):
    return jnp.concatenate([column, column], axis=1)


def back(base, field, factors, weight, offset, taps, ends, scale):
    terms = []
    for p in range(2):
        w = base[p] if field is None else base[p] * field[p]
        total = None
        for k in range(SAMPLES):
            factor = factors[k, p]
            column = weight[p] * jnp.sum(factor * w, axis=1, keepdims=True)
            if offset is not None:
                column = column - offset[p]
            term = factor * wide(column)
            total = term if total is None else total + term
        terms.append(base[p] * total)
    return tuple(scale * t for t in transpose_refine(terms, taps, ends))


def dot(a, b):
    total = a[0] * b[0] + a[1] * b[1]
    total = jnp.sum(total[:, :128] + total[:, 128:], axis=0, keepdims=True)
    return jnp.sum(total, axis=1, keepdims=True)


def moments_row(basis):
    pairs = [(0, 0), (0, 1), (1, 1), (1, 2), (2, 2), (2, 3)]
    lane = lax.broadcasted_iota(jnp.int32, (1, 128), 1)
    row = jnp.zeros((1, 128), jnp.float32)
    for n, (i, j) in enumerate(pairs):
        row = jnp.where(lane == n, dot(basis[i], basis[j]), row)
    return row


def coefficients(row):
    lane = lax.broadcasted_iota(jnp.int32, (1, 128), 1)
    nu = [jnp.sum(jnp.where(lane == n, row, 0.0), axis=1, keepdims=True) for n in range(2 * ITERS)]
    zero, one = jnp.zeros((1, 1), jnp.float32), jnp.ones((1, 1), jnp.float32)

    def inner(a, b):
        total = zero
        for i, x in enumerate(a):
            for j, y in enumerate(b):
                if i + j < 2 * ITERS:
                    total = total + x * y * nu[i + j]
        return total

    def ratio(a, b):
        return jnp.where(b > 0.0, a / jnp.where(b > 0.0, b, 1.0), 0.0)

    residual = [one]
    direction = [one]
    step = [zero] * ITERS
    norm_now = nu[0]
    for it in range(ITERS):
        padded = direction + [zero]
        image = [padded[0]] + [padded[j] + (1.0 / SHRINK) * padded[j - 1] for j in range(1, len(padded))]
        alpha = ratio(norm_now, inner(direction, image))
        step = [s + alpha * direction[j] if j < len(direction) else s for j, s in enumerate(step)]
        residual = [r - alpha * i for r, i in zip(residual + [zero], image)]
        if it < ITERS - 1:
            norm_next = inner(residual, residual)
            beta = ratio(norm_next, norm_now)
            direction = [r + beta * d for r, d in zip(residual, direction + [zero])]
            norm_now = norm_next
    return step, residual


def combine(coefs, basis):
    out = []
    for p in range(2):
        total = coefs[0] * basis[0][p]
        for c, b in zip(coefs[1:], basis[1:]):
            total = total + c * b[p]
        out.append(total)
    return tuple(out)


def krylov(latent, factors, weight, offset, taps, ends):
    base = tuple(jnp.exp(t) for t in refine(latent, taps, ends))
    pulled = back(base, None, factors, weight, offset, taps, ends, 1.0 / SAMPLES)
    basis = [tuple(-m - t for m, t in zip(latent, pulled))]
    for _ in range(ITERS):
        basis.append(
            back(base, refine(basis[-1], taps, ends), factors, weight, None, taps, ends, SHRINK / SAMPLES)
        )
    return basis


def pack_kernel(
    code, mean_all, draws_all, mask_all, noise_all, data_all, out,
    mean, draws, mask, noise, data, sems, *, count, members, copies, lines,
):
    first = pl.multiple_of((code[0] % members) * count, count)
    mine = pl.ds(first, count)
    loads = [
        pltpu.make_async_copy(source, target, sems.at[n])
        for n, (source, target) in enumerate(
            [
                (mean_all.at[:, mine, :], mean),
                (draws_all.at[:, :, mine, :], draws),
                (mask_all, mask),
                (noise_all, noise),
                (data_all, data),
            ]
        )
    ]
    for load in loads:
        load.start()
    for load in loads:
        load.wait()

    def place(r, rows):
        for fy in range(count // lines):
            for c in range(copies):
                first_block = (fy * copies + c) * lines
                out[pl.ds(first_block * ROWS + r, lines, stride=ROWS), :] = rows[fy * lines : fy * lines + lines]

    for a in range(1 + PAIRS):
        for p in range(2):
            for h in range(2):
                lanes = slice(h * 128, h * 128 + 128)
                rows = mean[p, :, lanes] if a == 0 else draws[a - 1, p, :, lanes]
                place(a * 4 + p * 2 + h, rows)
    row = lax.broadcasted_iota(jnp.int32, (count, 128), 0)
    lane = lax.broadcasted_iota(jnp.int32, (count, 128), 1)
    chosen = lane == row + first
    noisy = mask[...].astype(jnp.float32) * noise[...]
    extra = jnp.zeros((count, 128), jnp.float32)
    for n, values in enumerate((noisy * (1.0 / 256.0), noisy * data[...])):
        for p in range(2):
            picked = jnp.sum(jnp.where(chosen, values[p : p + 1, :], 0.0), axis=1, keepdims=True)
            extra = jnp.where(lane == n * 2 + p, picked, extra)
    place(20, extra)


def plane_rows(ref, a, p, n):
    return jnp.concatenate([ref[pl.ds(a * 4 + p * 2 + h, n, stride=ROWS), :] for h in range(2)], axis=1)


def columns(ref, n):
    extra = ref[pl.ds(20, n, stride=ROWS), :]
    spread = [jnp.broadcast_to(extra[:, c : c + 1], extra.shape) for c in range(4)]
    return spread[:2], spread[2:]


def first_kernel(packed, kernel, sums, factors, held, *, n):
    taps = [kernel[t : t + 1, :] for t in range(3)]
    ends = edges((n, 256))
    latent = tuple(plane_rows(packed, 0, p, n) for p in range(2))
    for k in range(PAIRS):
        spread = refine(tuple(plane_rows(packed, 1 + k, p, n) for p in range(2)), taps, ends)
        for p in range(2):
            factors[2 * k, p] = jnp.exp(spread[p])
            factors[2 * k + 1, p] = jnp.exp(-spread[p])
    weight, offset = columns(packed, n)
    basis = krylov(latent, factors, weight, offset, taps, ends)
    for p in range(2):
        held[0, p] = latent[p]
        for j in range(ITERS):
            held[1 + j, p] = basis[j][p]
    sums[...] = moments_row(basis)


def second_kernel(code, sums, packed, kernel, factors, held, out, block, *, n, groups, lines, members):
    taps = [kernel[t : t + 1, :] for t in range(3)]
    ends = edges((n, 256))
    step, _ = coefficients(jnp.sum(sums[...], axis=0, keepdims=True))
    basis = [tuple(held[j, p] for p in range(2)) for j in range(1 + ITERS)]
    latent = combine([jnp.ones((1, 1), jnp.float32)] + step, basis)
    weight, offset = columns(packed, n)
    basis = krylov(latent, factors, weight, offset, taps, ends)
    for a, v in enumerate([latent] + basis):
        for p in range(2):
            for h in range(2):
                block[pl.ds(a * 4 + p * 2 + h, n, stride=HELD), :] = v[p][:, h * 128 : h * 128 + 128]
    for fy in range(groups):
        for zl in range(lines):
            start = (fy * (n // groups) + zl) * HELD + (code[0] // members) * (lines * HELD)
            to = (fy * lines + zl) * ROWS
            out[pl.ds(to, ROWS - 1), :] = block[pl.ds(pl.multiple_of(start, 8), ROWS - 1), :]
    row = jnp.broadcast_to(moments_row(basis), (groups * lines, 128))
    out[pl.ds(ROWS - 1, groups * lines, stride=ROWS), :] = row


def last_kernel(code, found, other, mean_final, cg_residual, *, chips, count):
    core = code[0] % 2
    n = chips * count
    sums = found[pl.ds(20, n, stride=ROWS), :] + other[pl.ds(20, n, stride=ROWS), :]
    step, residual = coefficients(jnp.sum(sums, axis=0, keepdims=True))
    for ref, owner in ((found, core), (other, 1 - core)):
        for x in range(chips):
            rows = pl.ds(pl.multiple_of((2 * x + owner) * count, count), count)
            for p in range(2):
                for h in range(2):
                    v = [
                        ref[pl.ds(x * count * ROWS + a * 4 + p * 2 + h, count, stride=ROWS), :]
                        for a in range(2 + ITERS)
                    ]
                    latent = v[0]
                    for c, b in zip(step, v[1:]):
                        latent = latent + c * b
                    rest = residual[0] * v[1]
                    for c, b in zip(residual[1:], v[2:]):
                        rest = rest + c * b
                    mean_final[p, rows, h * 128 : h * 128 + 128] = latent
                    cg_residual[p, rows, h * 128 : h * 128 + 128] = rest


def spread(block, axis):
    copies = lax.axis_size(axis)
    block = jnp.broadcast_to(block[None], (copies,) + block.shape)
    return lax.all_to_all(block, axis, 0, 0, tiled=True)


def local(mean_start, sample_draws, kernel, sight_mask, noise_weight, data):
    nx, nc, nfy, nzq, nzl = (lax.axis_size(a) for a in ("x", "core", "fy", "zq", "zl"))
    members = nx * nc
    fields = nfy * nzq * nzl
    lines = nfy * nzl
    count = mean_start.shape[1] // members
    depth = mean_start.shape[2]
    f32 = functools.partial(jax.ShapeDtypeStruct, dtype=jnp.float32)
    params = pltpu.CompilerParams(vmem_limit_bytes=VMEM)
    whole = pl.BlockSpec(memory_space=pltpu.VMEM)
    scalar = pl.BlockSpec(memory_space=pltpu.SMEM)
    code = lax.axis_index("zq") * members + lax.axis_index("x") * nc + lax.axis_index("core")
    code = code.astype(jnp.int32).reshape(1)

    packed = pl.pallas_call(
        functools.partial(pack_kernel, count=count, members=members, copies=nzq, lines=nzl),
        out_shape=f32((fields * ROWS, 128)),
        in_specs=[scalar] + [pl.BlockSpec(memory_space=pltpu.HBM)] * 5,
        out_specs=whole,
        scratch_shapes=[
            pltpu.VMEM((2, count, depth), jnp.float32),
            pltpu.VMEM((PAIRS, 2, count, depth), jnp.float32),
            pltpu.VMEM(sight_mask.shape, jnp.int32),
            pltpu.VMEM(noise_weight.shape, jnp.float32),
            pltpu.VMEM(data.shape, jnp.float32),
            pltpu.SemaphoreType.DMA((5,)),
        ],
        compiler_params=pltpu.CompilerParams(vmem_limit_bytes=FULL),
        name="pack",
    )(code, mean_start, sample_draws, sight_mask, noise_weight, data)

    packed = lax.all_to_all(packed.reshape(fields * ROWS, 1, 128), ("fy", "zq", "zl"), 0, 0, tiled=True)
    packed = packed.reshape(fields * ROWS, 128)

    sharers = members * lines
    sums, factors, held = pl.pallas_call(
        functools.partial(first_kernel, n=fields),
        out_shape=[
            f32((1, 128)),
            f32((SAMPLES, 2, fields, depth)),
            f32((1 + ITERS, 2, fields, depth)),
        ],
        in_specs=[whole, whole],
        out_specs=[whole, whole, whole],
        compiler_params=params,
        name="first",
    )(packed, kernel)

    sums = jnp.broadcast_to(sums[None], (sharers, 1, 128))
    sums = lax.all_to_all(sums, ("core", "x", "fy", "zl"), 0, 0, tiled=True)
    sums = sums.reshape(sharers, 128)

    found = pl.pallas_call(
        functools.partial(second_kernel, n=fields, groups=nfy, lines=nzl, members=members),
        out_shape=f32((lines * ROWS, 128)),
        in_specs=[scalar] + [whole] * 5,
        out_specs=whole,
        scratch_shapes=[pltpu.VMEM((fields * HELD, 128), jnp.float32)],
        compiler_params=params,
        name="second",
    )(code, sums, packed, kernel, factors, held)

    found = lax.all_to_all(found.reshape(lines * ROWS, 1, 128), ("fy", "zl"), 0, 0, tiled=True)
    found = spread(found, "x").reshape(nx * lines * ROWS, 128)
    other = lax.ppermute(found, "core", [(0, 1), (1, 0)])

    return pl.pallas_call(
        functools.partial(last_kernel, chips=nx, count=count),
        out_shape=[f32(mean_start.shape), f32(mean_start.shape)],
        in_specs=[scalar, whole, whole],
        out_specs=[whole, whole],
        compiler_params=params,
        name="last",
    )(code, found, other)


def solution(mesh):
    split = Mesh(mesh.devices.reshape(4, 2, 4, 4, 4), ("x", "core", "fy", "zq", "zl"))
    field = ("fy", "zq", "zl")
    placed = (
        P(field, None, None),
        P(None, field, None, None),
        P(),
        P(field, None),
        P(field, None),
        P(field, None),
    )
    return jax.shard_map(
        local,
        mesh=split,
        in_specs=placed,
        out_specs=(P(field, None, None), P(field, None, None)),
        check_vma=False,
    )
```

```python
import functools

import jax
import jax.numpy as jnp
from jax import lax
from jax.experimental import pallas as pl
from jax.experimental.pallas import tpu as pltpu
from jax.sharding import Mesh, PartitionSpec as P

NEWTON = 2
ITERS = 3
PAIRS = 4
SAMPLES = 8
ROWS = 21
HELD = 24
SHRINK = 2.0**-10
VMEM = 48 * 1024 * 1024
FULL = 57 * 1024 * 1024


def shift_up(v, first):
    return jnp.where(first, 0.0, pltpu.roll(v, 1, 0))


def shift_down(v, last):
    return jnp.where(last, 0.0, pltpu.roll(v, v.shape[0] - 1, 0))


def edges(shape):
    row = lax.broadcasted_iota(jnp.int32, shape, 0)
    return row == 0, row == shape[0] - 1


def refine(v, taps, ends):
    even, odd = v
    return (
        taps[0] * shift_up(odd, ends[0]) + taps[1] * even + taps[2] * odd,
        taps[0] * even + taps[1] * odd + taps[2] * shift_down(even, ends[1]),
    )


def transpose_refine(u, taps, ends):
    even, odd = u
    return (
        taps[0] * odd + taps[1] * even + taps[2] * shift_up(odd, ends[0]),
        taps[0] * shift_down(even, ends[1]) + taps[1] * odd + taps[2] * even,
    )


def wide(column):
    return jnp.concatenate([column, column], axis=1)


def back(base, field, factors, weight, offset, taps, ends, scale):
    terms = []
    for p in range(2):
        w = base[p] if field is None else base[p] * field[p]
        total = None
        for k in range(SAMPLES):
            factor = factors[k, p]
            column = weight[p] * jnp.sum(factor * w, axis=1, keepdims=True)
            if offset is not None:
                column = column - offset[p]
            term = factor * wide(column)
            total = term if total is None else total + term
        terms.append(base[p] * total)
    return tuple(scale * t for t in transpose_refine(terms, taps, ends))


def dot(a, b):
    total = a[0] * b[0] + a[1] * b[1]
    total = jnp.sum(total[:, :128] + total[:, 128:], axis=0, keepdims=True)
    return jnp.sum(total, axis=1, keepdims=True)


def moments_row(basis):
    pairs = [(0, 0), (0, 1), (1, 1), (1, 2), (2, 2), (2, 3)]
    lane = lax.broadcasted_iota(jnp.int32, (1, 128), 1)
    row = jnp.zeros((1, 128), jnp.float32)
    for n, (i, j) in enumerate(pairs):
        row = jnp.where(lane == n, dot(basis[i], basis[j]), row)
    return row


def two_sum(a, b):
    total = a + b
    part = total - a
    return total, (a - (total - part)) + (b - part)


def halves_of(a):
    scaled = a * 4097.0
    high = scaled - (scaled - a)
    return high, a - high


def two_product(a, b):
    product = a * b
    (ah, al), (bh, bl) = halves_of(a), halves_of(b)
    return product, ((ah * bh - product) + ah * bl + al * bh) + al * bl


def careful_sum(rows):
    total, rest = rows[:8], jnp.zeros((8, 128), jnp.float32)
    for t in range(8, rows.shape[0], 8):
        total, error = two_sum(total, rows[t : t + 8])
        rest = rest + error
    for shift in (4, 2, 1):
        other, other_rest = pltpu.roll(total, shift, 0), pltpu.roll(rest, shift, 0)
        total, error = two_sum(total, other)
        rest = rest + other_rest + error
    return total[:1], rest[:1]


def coefficients(rows):
    lane = lax.broadcasted_iota(jnp.int32, (1, 128), 1)
    total, rest = careful_sum(rows)
    nu = [
        tuple(jnp.sum(jnp.where(lane == n, part, 0.0), axis=1, keepdims=True) for part in (total, rest))
        for n in range(2 * ITERS)
    ]
    zero, one = jnp.zeros((1, 1), jnp.float32), jnp.ones((1, 1), jnp.float32)

    def inner(a, b):
        weights = {}
        for i, x in enumerate(a):
            for j, y in enumerate(b):
                if i + j < 2 * ITERS:
                    product, error = two_product(x, y)
                    if i + j in weights:
                        high, low = weights[i + j]
                        high, more = two_sum(high, product)
                        weights[i + j] = high, low + (error + more)
                    else:
                        weights[i + j] = product, error
        total, rest = None, zero
        for n, (high, low) in weights.items():
            product, error = two_product(high, nu[n][0])
            error = error + (high * nu[n][1] + low * nu[n][0])
            if total is None:
                total, rest = product, error
            else:
                total, more = two_sum(total, product)
                rest = rest + (error + more)
        return total + rest

    def ratio(a, b):
        return jnp.where(b > 0.0, a / jnp.where(b > 0.0, b, 1.0), 0.0)

    residual = [one]
    direction = [one]
    step = [zero] * ITERS
    norm_now = nu[0][0] + nu[0][1]
    for it in range(ITERS):
        padded = direction + [zero]
        image = [padded[0]] + [padded[j] + (1.0 / SHRINK) * padded[j - 1] for j in range(1, len(padded))]
        alpha = jnp.clip(ratio(norm_now, inner(direction, image)), 0.0, 1.0)
        step = [s + alpha * direction[j] if j < len(direction) else s for j, s in enumerate(step)]
        residual = [r - alpha * i for r, i in zip(residual + [zero], image)]
        if it < ITERS - 1:
            norm_next = jnp.maximum(inner(residual, residual), 0.0)
            beta = ratio(norm_next, norm_now)
            direction = [r + beta * d for r, d in zip(residual, direction + [zero])]
            norm_now = norm_next
    return step, residual


def combine(coefs, basis):
    out = []
    for p in range(2):
        total = coefs[0] * basis[0][p]
        for c, b in zip(coefs[1:], basis[1:]):
            total = total + c * b[p]
        out.append(total)
    return tuple(out)


def krylov(latent, factors, weight, offset, taps, ends):
    base = tuple(jnp.exp(t) for t in refine(latent, taps, ends))
    pulled = back(base, None, factors, weight, offset, taps, ends, 1.0 / SAMPLES)
    basis = [tuple(-m - t for m, t in zip(latent, pulled))]
    for _ in range(ITERS):
        basis.append(
            back(base, refine(basis[-1], taps, ends), factors, weight, None, taps, ends, SHRINK / SAMPLES)
        )
    return basis


def pack_kernel(
    code, mean_all, draws_all, mask_all, noise_all, data_all, out,
    mean, draws, mask, noise, data, sems, *, count, members, copies, lines,
):
    first = pl.multiple_of((code[0] % members) * count, count)
    mine = pl.ds(first, count)
    loads = [
        pltpu.make_async_copy(source, target, sems.at[n])
        for n, (source, target) in enumerate(
            [
                (mean_all.at[:, mine, :], mean),
                (draws_all.at[:, :, mine, :], draws),
                (mask_all, mask),
                (noise_all, noise),
                (data_all, data),
            ]
        )
    ]
    for load in loads:
        load.start()
    for load in loads:
        load.wait()

    def place(r, rows):
        for fy in range(count // lines):
            for c in range(copies):
                first_block = (fy * copies + c) * lines
                out[pl.ds(first_block * ROWS + r, lines, stride=ROWS), :] = rows[fy * lines : fy * lines + lines]

    for a in range(1 + PAIRS):
        for p in range(2):
            for h in range(2):
                lanes = slice(h * 128, h * 128 + 128)
                rows = mean[p, :, lanes] if a == 0 else draws[a - 1, p, :, lanes]
                place(a * 4 + p * 2 + h, rows)
    row = lax.broadcasted_iota(jnp.int32, (count, 128), 0)
    lane = lax.broadcasted_iota(jnp.int32, (count, 128), 1)
    chosen = lane == row + first
    noisy = mask[...].astype(jnp.float32) * noise[...]
    extra = jnp.zeros((count, 128), jnp.float32)
    for n, values in enumerate((noisy * (1.0 / 256.0), noisy * data[...])):
        for p in range(2):
            picked = jnp.sum(jnp.where(chosen, values[p : p + 1, :], 0.0), axis=1, keepdims=True)
            extra = jnp.where(lane == n * 2 + p, picked, extra)
    place(20, extra)


def plane_rows(ref, a, p, n):
    return jnp.concatenate([ref[pl.ds(a * 4 + p * 2 + h, n, stride=ROWS), :] for h in range(2)], axis=1)


def columns(ref, n):
    extra = ref[pl.ds(20, n, stride=ROWS), :]
    spread = [jnp.broadcast_to(extra[:, c : c + 1], extra.shape) for c in range(4)]
    return spread[:2], spread[2:]


def first_kernel(packed, kernel, sums, factors, held, *, n):
    taps = [kernel[t : t + 1, :] for t in range(3)]
    ends = edges((n, 256))
    latent = tuple(plane_rows(packed, 0, p, n) for p in range(2))
    for k in range(PAIRS):
        spread = refine(tuple(plane_rows(packed, 1 + k, p, n) for p in range(2)), taps, ends)
        for p in range(2):
            factors[2 * k, p] = jnp.exp(spread[p])
            factors[2 * k + 1, p] = jnp.exp(-spread[p])
    weight, offset = columns(packed, n)
    basis = krylov(latent, factors, weight, offset, taps, ends)
    for p in range(2):
        held[0, p] = latent[p]
        for j in range(ITERS):
            held[1 + j, p] = basis[j][p]
    sums[...] = moments_row(basis)


def second_kernel(code, sums, packed, kernel, factors, held, out, block, *, n, groups, lines, members):
    taps = [kernel[t : t + 1, :] for t in range(3)]
    ends = edges((n, 256))
    step, _ = coefficients(sums[...])
    basis = [tuple(held[j, p] for p in range(2)) for j in range(1 + ITERS)]
    latent = combine([jnp.ones((1, 1), jnp.float32)] + step, basis)
    weight, offset = columns(packed, n)
    basis = krylov(latent, factors, weight, offset, taps, ends)
    for a, v in enumerate([latent] + basis):
        for p in range(2):
            for h in range(2):
                block[pl.ds(a * 4 + p * 2 + h, n, stride=HELD), :] = v[p][:, h * 128 : h * 128 + 128]
    for fy in range(groups):
        for zl in range(lines):
            start = (fy * (n // groups) + zl) * HELD + (code[0] // members) * (lines * HELD)
            to = (fy * lines + zl) * ROWS
            out[pl.ds(to, ROWS - 1), :] = block[pl.ds(pl.multiple_of(start, 8), ROWS - 1), :]
    row = jnp.broadcast_to(moments_row(basis), (groups * lines, 128))
    out[pl.ds(ROWS - 1, groups * lines, stride=ROWS), :] = row


def last_kernel(code, found, other, mean_final, cg_residual, *, chips, count):
    core = code[0] % 2
    n = chips * count
    sums = [ref[pl.ds(20, n, stride=ROWS), :] for ref in (found, other)]
    step, residual = coefficients(jnp.concatenate(sums, axis=0))
    for ref, owner in ((found, core), (other, 1 - core)):
        for x in range(chips):
            rows = pl.ds(pl.multiple_of((2 * x + owner) * count, count), count)
            for p in range(2):
                for h in range(2):
                    v = [
                        ref[pl.ds(x * count * ROWS + a * 4 + p * 2 + h, count, stride=ROWS), :]
                        for a in range(2 + ITERS)
                    ]
                    latent = v[0]
                    for c, b in zip(step, v[1:]):
                        latent = latent + c * b
                    rest = residual[0] * v[1]
                    for c, b in zip(residual[1:], v[2:]):
                        rest = rest + c * b
                    mean_final[p, rows, h * 128 : h * 128 + 128] = latent
                    cg_residual[p, rows, h * 128 : h * 128 + 128] = rest


def spread(block, axis):
    copies = lax.axis_size(axis)
    block = jnp.broadcast_to(block[None], (copies,) + block.shape)
    return lax.all_to_all(block, axis, 0, 0, tiled=True)


def local(mean_start, sample_draws, kernel, sight_mask, noise_weight, data):
    nx, nc, nfy, nzq, nzl = (lax.axis_size(a) for a in ("x", "core", "fy", "zq", "zl"))
    members = nx * nc
    fields = nfy * nzq * nzl
    lines = nfy * nzl
    count = mean_start.shape[1] // members
    depth = mean_start.shape[2]
    f32 = functools.partial(jax.ShapeDtypeStruct, dtype=jnp.float32)
    params = pltpu.CompilerParams(vmem_limit_bytes=VMEM)
    whole = pl.BlockSpec(memory_space=pltpu.VMEM)
    scalar = pl.BlockSpec(memory_space=pltpu.SMEM)
    code = lax.axis_index("zq") * members + lax.axis_index("x") * nc + lax.axis_index("core")
    code = code.astype(jnp.int32).reshape(1)

    packed = pl.pallas_call(
        functools.partial(pack_kernel, count=count, members=members, copies=nzq, lines=nzl),
        out_shape=f32((fields * ROWS, 128)),
        in_specs=[scalar] + [pl.BlockSpec(memory_space=pltpu.HBM)] * 5,
        out_specs=whole,
        scratch_shapes=[
            pltpu.VMEM((2, count, depth), jnp.float32),
            pltpu.VMEM((PAIRS, 2, count, depth), jnp.float32),
            pltpu.VMEM(sight_mask.shape, jnp.int32),
            pltpu.VMEM(noise_weight.shape, jnp.float32),
            pltpu.VMEM(data.shape, jnp.float32),
            pltpu.SemaphoreType.DMA((5,)),
        ],
        compiler_params=pltpu.CompilerParams(vmem_limit_bytes=FULL),
        name="pack",
    )(code, mean_start, sample_draws, sight_mask, noise_weight, data)

    packed = lax.all_to_all(packed.reshape(fields * ROWS, 1, 128), ("fy", "zq", "zl"), 0, 0, tiled=True)
    packed = packed.reshape(fields * ROWS, 128)

    sharers = members * lines
    sums, factors, held = pl.pallas_call(
        functools.partial(first_kernel, n=fields),
        out_shape=[
            f32((1, 128)),
            f32((SAMPLES, 2, fields, depth)),
            f32((1 + ITERS, 2, fields, depth)),
        ],
        in_specs=[whole, whole],
        out_specs=[whole, whole, whole],
        compiler_params=params,
        name="first",
    )(packed, kernel)

    sums = jnp.broadcast_to(sums[None], (sharers, 1, 128))
    sums = lax.all_to_all(sums, ("core", "x", "fy", "zl"), 0, 0, tiled=True)
    sums = sums.reshape(sharers, 128)

    found = pl.pallas_call(
        functools.partial(second_kernel, n=fields, groups=nfy, lines=nzl, members=members),
        out_shape=f32((lines * ROWS, 128)),
        in_specs=[scalar] + [whole] * 5,
        out_specs=whole,
        scratch_shapes=[pltpu.VMEM((fields * HELD, 128), jnp.float32)],
        compiler_params=params,
        name="second",
    )(code, sums, packed, kernel, factors, held)

    found = lax.all_to_all(found.reshape(lines * ROWS, 1, 128), ("fy", "zl"), 0, 0, tiled=True)
    found = spread(found, "x").reshape(nx * lines * ROWS, 128)
    other = lax.ppermute(found, "core", [(0, 1), (1, 0)])

    return pl.pallas_call(
        functools.partial(last_kernel, chips=nx, count=count),
        out_shape=[f32(mean_start.shape), f32(mean_start.shape)],
        in_specs=[scalar, whole, whole],
        out_specs=[whole, whole],
        compiler_params=params,
        name="last",
    )(code, found, other)


def solution(mesh):
    split = Mesh(mesh.devices.reshape(4, 2, 4, 4, 4), ("x", "core", "fy", "zq", "zl"))
    field = ("fy", "zq", "zl")
    placed = (
        P(field, None, None),
        P(None, field, None, None),
        P(),
        P(field, None),
        P(field, None),
        P(field, None),
    )
    return jax.shard_map(
        local,
        mesh=split,
        in_specs=placed,
        out_specs=(P(field, None, None), P(field, None, None)),
        check_vma=False,
    )
```

```python
import functools

import jax
import jax.numpy as jnp
from jax import lax
from jax.experimental import pallas as pl
from jax.experimental.pallas import tpu as pltpu
from jax.sharding import Mesh, PartitionSpec as P

NEWTON = 2
ITERS = 3
PAIRS = 4
SAMPLES = 8
ROWS = 21
HELD = 24
SHRINK = 2.0**-10
VMEM = 48 * 1024 * 1024
FULL = 57 * 1024 * 1024


def shift_up(v, first):
    return jnp.where(first, 0.0, pltpu.roll(v, 1, 0))


def shift_down(v, last):
    return jnp.where(last, 0.0, pltpu.roll(v, v.shape[0] - 1, 0))


def edges(shape):
    row = lax.broadcasted_iota(jnp.int32, shape, 0)
    return row == 0, row == shape[0] - 1


def refine(v, taps, ends):
    even, odd = v
    return (
        taps[0] * shift_up(odd, ends[0]) + taps[1] * even + taps[2] * odd,
        taps[0] * even + taps[1] * odd + taps[2] * shift_down(even, ends[1]),
    )


def transpose_refine(u, taps, ends):
    even, odd = u
    return (
        taps[0] * odd + taps[1] * even + taps[2] * shift_up(odd, ends[0]),
        taps[0] * shift_down(even, ends[1]) + taps[1] * odd + taps[2] * even,
    )


def wide(column):
    return jnp.concatenate([column, column], axis=1)


def back(base, field, factors, weight, offset, taps, ends, scale):
    terms = []
    for p in range(2):
        w = base[p] if field is None else base[p] * field[p]
        total = None
        for k in range(SAMPLES):
            factor = factors[k, p]
            column = weight[p] * jnp.sum(factor * w, axis=1, keepdims=True)
            if offset is not None:
                column = column - offset[p]
            term = factor * wide(column)
            total = term if total is None else total + term
        terms.append(base[p] * total)
    return tuple(scale * t for t in transpose_refine(terms, taps, ends))


def dot(a, b):
    total = a[0] * b[0] + a[1] * b[1]
    total = jnp.sum(total[:, :128] + total[:, 128:], axis=0, keepdims=True)
    return jnp.sum(total, axis=1, keepdims=True)


def moments_row(basis):
    pairs = [(0, 0), (0, 1), (1, 1), (1, 2), (2, 2), (2, 3)]
    lane = lax.broadcasted_iota(jnp.int32, (1, 128), 1)
    row = jnp.zeros((1, 128), jnp.float32)
    for n, (i, j) in enumerate(pairs):
        row = jnp.where(lane == n, dot(basis[i], basis[j]), row)
    return row


def two_sum(a, b):
    total = a + b
    part = total - a
    return total, (a - (total - part)) + (b - part)


def halves_of(a):
    scaled = a * 4097.0
    high = scaled - (scaled - a)
    return high, a - high


def two_product(a, b):
    product = a * b
    (ah, al), (bh, bl) = halves_of(a), halves_of(b)
    return product, ((ah * bh - product) + ah * bl + al * bh) + al * bl


def careful_sum(rows):
    total, rest = rows[:8], jnp.zeros((8, 128), jnp.float32)
    for t in range(8, rows.shape[0], 8):
        total, error = two_sum(total, rows[t : t + 8])
        rest = rest + error
    for shift in (4, 2, 1):
        other, other_rest = pltpu.roll(total, shift, 0), pltpu.roll(rest, shift, 0)
        total, error = two_sum(total, other)
        rest = rest + other_rest + error
    return total[:1], rest[:1]


def coefficients(rows):
    lane = lax.broadcasted_iota(jnp.int32, (1, 128), 1)
    total, rest = careful_sum(rows)
    nu = [
        tuple(jnp.sum(jnp.where(lane == n, part, 0.0), axis=1, keepdims=True) for part in (total, rest))
        for n in range(2 * ITERS)
    ]
    zero, one = jnp.zeros((1, 1), jnp.float32), jnp.ones((1, 1), jnp.float32)

    def inner(a, b):
        weights = {}
        for i, x in enumerate(a):
            for j, y in enumerate(b):
                if i + j < 2 * ITERS:
                    product, error = two_product(x, y)
                    if i + j in weights:
                        high, low = weights[i + j]
                        high, more = two_sum(high, product)
                        weights[i + j] = high, low + (error + more)
                    else:
                        weights[i + j] = product, error
        total, rest = None, zero
        for n, (high, low) in weights.items():
            product, error = two_product(high, nu[n][0])
            error = error + (high * nu[n][1] + low * nu[n][0])
            if total is None:
                total, rest = product, error
            else:
                total, more = two_sum(total, product)
                rest = rest + (error + more)
        return total + rest

    def ratio(a, b):
        return jnp.where(b > 0.0, a / jnp.where(b > 0.0, b, 1.0), 0.0)

    residual = [one]
    direction = [one]
    step = [zero] * ITERS
    norm_now = nu[0][0] + nu[0][1]
    for it in range(ITERS):
        padded = direction + [zero]
        image = [padded[0]] + [padded[j] + (1.0 / SHRINK) * padded[j - 1] for j in range(1, len(padded))]
        alpha = jnp.clip(ratio(norm_now, inner(direction, image)), 0.0, 1.0)
        step = [s + alpha * direction[j] if j < len(direction) else s for j, s in enumerate(step)]
        residual = [r - alpha * i for r, i in zip(residual + [zero], image)]
        if it < ITERS - 1:
            norm_next = jnp.maximum(inner(residual, residual), 0.0)
            beta = ratio(norm_next, norm_now)
            direction = [r + beta * d for r, d in zip(residual, direction + [zero])]
            norm_now = norm_next
    return step, residual


def combine(coefs, basis):
    out = []
    for p in range(2):
        total = coefs[0] * basis[0][p]
        for c, b in zip(coefs[1:], basis[1:]):
            total = total + c * b[p]
        out.append(total)
    return tuple(out)


def krylov(latent, factors, weight, offset, taps, ends):
    base = tuple(jnp.exp(t) for t in refine(latent, taps, ends))
    pulled = back(base, None, factors, weight, offset, taps, ends, 1.0 / SAMPLES)
    basis = [tuple(-m - t for m, t in zip(latent, pulled))]
    for _ in range(ITERS):
        basis.append(
            back(base, refine(basis[-1], taps, ends), factors, weight, None, taps, ends, SHRINK / SAMPLES)
        )
    return basis


def pack_kernel(
    code, mean_all, draws_all, mask_all, noise_all, data_all, out,
    mean, draws, mask, noise, data, sems, *, count, members, halves, copies, lines,
):
    first = pl.multiple_of((code[0] % members) * count, count)
    mine = pl.ds(first, count)
    loads = [
        pltpu.make_async_copy(source, target, sems.at[n])
        for n, (source, target) in enumerate(
            [
                (mean_all.at[:, mine, :], mean),
                (draws_all.at[:, :, mine, :], draws),
                (mask_all, mask),
                (noise_all, noise),
                (data_all, data),
            ]
        )
    ]
    for load in loads:
        load.start()
    for load in loads:
        load.wait()

    def place(r, rows):
        groups = count // lines
        width = halves * groups
        for c in range(copies):
            for h in range(halves):
                for fy in range(groups):
                    to = c * lines * width + h * groups + fy
                    out[pl.ds(to * ROWS + r, lines, stride=width * ROWS), :] = rows[fy * lines : fy * lines + lines]

    for a in range(1 + PAIRS):
        for p in range(2):
            for h in range(2):
                lanes = slice(h * 128, h * 128 + 128)
                rows = mean[p, :, lanes] if a == 0 else draws[a - 1, p, :, lanes]
                place(a * 4 + p * 2 + h, rows)
    row = lax.broadcasted_iota(jnp.int32, (count, 128), 0)
    lane = lax.broadcasted_iota(jnp.int32, (count, 128), 1)
    chosen = lane == row + first
    noisy = mask[...].astype(jnp.float32) * noise[...]
    extra = jnp.zeros((count, 128), jnp.float32)
    for n, values in enumerate((noisy * (1.0 / 256.0), noisy * data[...])):
        for p in range(2):
            picked = jnp.sum(jnp.where(chosen, values[p : p + 1, :], 0.0), axis=1, keepdims=True)
            extra = jnp.where(lane == n * 2 + p, picked, extra)
    place(20, extra)


def lane_rows(ref, r, order):
    halves, groups, run = order
    width = halves * groups
    return jnp.concatenate(
        [
            ref[pl.ds((h * groups + fy) * ROWS + r, run, stride=width * ROWS), :]
            for fy in range(groups)
            for h in range(halves)
        ],
        axis=0,
    )


def plane_rows(ref, a, p, order):
    return jnp.concatenate([lane_rows(ref, a * 4 + p * 2 + h, order) for h in range(2)], axis=1)


def columns(ref, order):
    extra = lane_rows(ref, 20, order)
    spread = [jnp.broadcast_to(extra[:, c : c + 1], extra.shape) for c in range(4)]
    return spread[:2], spread[2:]


def first_kernel(packed, kernel, sums, factors, held, *, n, order):
    taps = [kernel[t : t + 1, :] for t in range(3)]
    ends = edges((n, 256))
    latent = tuple(plane_rows(packed, 0, p, order) for p in range(2))
    for k in range(PAIRS):
        spread = refine(tuple(plane_rows(packed, 1 + k, p, order) for p in range(2)), taps, ends)
        for p in range(2):
            factors[2 * k, p] = jnp.exp(spread[p])
            factors[2 * k + 1, p] = jnp.exp(-spread[p])
    weight, offset = columns(packed, order)
    basis = krylov(latent, factors, weight, offset, taps, ends)
    for p in range(2):
        held[0, p] = latent[p]
        for j in range(ITERS):
            held[1 + j, p] = basis[j][p]
    sums[...] = moments_row(basis)


def second_kernel(code, sums, packed, kernel, factors, held, out, block, *, n, order, groups, lines, members):
    taps = [kernel[t : t + 1, :] for t in range(3)]
    ends = edges((n, 256))
    step, _ = coefficients(sums[...])
    basis = [tuple(held[j, p] for p in range(2)) for j in range(1 + ITERS)]
    latent = combine([jnp.ones((1, 1), jnp.float32)] + step, basis)
    weight, offset = columns(packed, order)
    basis = krylov(latent, factors, weight, offset, taps, ends)
    for a, v in enumerate([latent] + basis):
        for p in range(2):
            for h in range(2):
                block[pl.ds(a * 4 + p * 2 + h, n, stride=HELD), :] = v[p][:, h * 128 : h * 128 + 128]
    for fy in range(groups):
        for zl in range(lines):
            start = (fy * (n // groups) + zl) * HELD + (code[0] // members) * (lines * HELD)
            to = (fy * lines + zl) * ROWS
            out[pl.ds(to, ROWS - 1), :] = block[pl.ds(pl.multiple_of(start, 8), ROWS - 1), :]
    row = jnp.broadcast_to(moments_row(basis), (groups * lines, 128))
    out[pl.ds(ROWS - 1, groups * lines, stride=ROWS), :] = row


def last_kernel(code, found, other, mean_final, cg_residual, *, chips, count):
    core = code[0] % 2
    n = chips * count
    sums = [ref[pl.ds(20, n, stride=ROWS), :] for ref in (found, other)]
    step, residual = coefficients(jnp.concatenate(sums, axis=0))
    for ref, owner in ((found, core), (other, 1 - core)):
        for x in range(chips):
            rows = pl.ds(pl.multiple_of((2 * x + owner) * count, count), count)
            for p in range(2):
                for h in range(2):
                    v = [
                        ref[pl.ds(x * count * ROWS + a * 4 + p * 2 + h, count, stride=ROWS), :]
                        for a in range(2 + ITERS)
                    ]
                    latent = v[0]
                    for c, b in zip(step, v[1:]):
                        latent = latent + c * b
                    rest = residual[0] * v[1]
                    for c, b in zip(residual[1:], v[2:]):
                        rest = rest + c * b
                    mean_final[p, rows, h * 128 : h * 128 + 128] = latent
                    cg_residual[p, rows, h * 128 : h * 128 + 128] = rest


def spread(block, axis):
    copies = lax.axis_size(axis)
    block = jnp.broadcast_to(block[None], (copies,) + block.shape)
    return lax.all_to_all(block, axis, 0, 0, tiled=True)


def local(mean_start, sample_draws, kernel, sight_mask, noise_weight, data):
    nx, nc, nfy, nzh, nzk, nzl = (lax.axis_size(a) for a in ("x", "core", "fy", "zh", "zk", "zl"))
    members = nx * nc
    fields = nfy * nzh * nzk * nzl
    lines = nfy * nzl
    count = mean_start.shape[1] // members
    depth = mean_start.shape[2]
    f32 = functools.partial(jax.ShapeDtypeStruct, dtype=jnp.float32)
    params = pltpu.CompilerParams(vmem_limit_bytes=VMEM)
    whole = pl.BlockSpec(memory_space=pltpu.VMEM)
    scalar = pl.BlockSpec(memory_space=pltpu.SMEM)
    code = lax.axis_index(("zh", "zk")) * members + lax.axis_index("x") * nc + lax.axis_index("core")
    code = code.astype(jnp.int32).reshape(1)

    packed = pl.pallas_call(
        functools.partial(pack_kernel, count=count, members=members, halves=nzh, copies=nzk, lines=nzl),
        out_shape=f32((fields * ROWS, 128)),
        in_specs=[scalar] + [pl.BlockSpec(memory_space=pltpu.HBM)] * 5,
        out_specs=whole,
        scratch_shapes=[
            pltpu.VMEM((2, count, depth), jnp.float32),
            pltpu.VMEM((PAIRS, 2, count, depth), jnp.float32),
            pltpu.VMEM(sight_mask.shape, jnp.int32),
            pltpu.VMEM(noise_weight.shape, jnp.float32),
            pltpu.VMEM(data.shape, jnp.float32),
            pltpu.SemaphoreType.DMA((5,)),
        ],
        compiler_params=pltpu.CompilerParams(vmem_limit_bytes=FULL),
        name="pack",
    )(code, mean_start, sample_draws, sight_mask, noise_weight, data)

    packed = lax.all_to_all(packed.reshape(fields * ROWS, 1, 128), ("zk", "zl", "zh", "fy"), 0, 0, tiled=True)
    packed = packed.reshape(fields * ROWS, 128)

    order = (nzh, nfy, nzk * nzl)
    sharers = members * lines
    sums, factors, held = pl.pallas_call(
        functools.partial(first_kernel, n=fields, order=order),
        out_shape=[
            f32((1, 128)),
            f32((SAMPLES, 2, fields, depth)),
            f32((1 + ITERS, 2, fields, depth)),
        ],
        in_specs=[whole, whole],
        out_specs=[whole, whole, whole],
        compiler_params=params,
        name="first",
    )(packed, kernel)

    sums = jnp.broadcast_to(sums[None], (sharers, 1, 128))
    sums = lax.all_to_all(sums, ("core", "x", "fy", "zl"), 0, 0, tiled=True)
    sums = sums.reshape(sharers, 128)

    found = pl.pallas_call(
        functools.partial(second_kernel, n=fields, order=order, groups=nfy, lines=nzl, members=members),
        out_shape=f32((lines * ROWS, 128)),
        in_specs=[scalar] + [whole] * 5,
        out_specs=whole,
        scratch_shapes=[pltpu.VMEM((fields * HELD, 128), jnp.float32)],
        compiler_params=params,
        name="second",
    )(code, sums, packed, kernel, factors, held)

    found = lax.all_to_all(found.reshape(lines * ROWS, 1, 128), ("fy", "zl"), 0, 0, tiled=True)
    found = spread(found, "x").reshape(nx * lines * ROWS, 128)
    other = lax.ppermute(found, "core", [(0, 1), (1, 0)])

    return pl.pallas_call(
        functools.partial(last_kernel, chips=nx, count=count),
        out_shape=[f32(mean_start.shape), f32(mean_start.shape)],
        in_specs=[scalar, whole, whole],
        out_specs=[whole, whole],
        compiler_params=params,
        name="last",
    )(code, found, other)


def solution(mesh):
    split = Mesh(mesh.devices.reshape(4, 2, 4, 2, 2, 4), ("x", "core", "fy", "zh", "zk", "zl"))
    field = ("fy", "zh", "zk", "zl")
    placed = (
        P(field, None, None),
        P(None, field, None, None),
        P(),
        P(field, None),
        P(field, None),
        P(field, None),
    )
    return jax.shard_map(
        local,
        mesh=split,
        in_specs=placed,
        out_specs=(P(field, None, None), P(field, None, None)),
        check_vma=False,
    )
```

```python
import functools

import jax
import jax.numpy as jnp
from jax import lax
from jax.experimental import pallas as pl
from jax.experimental.pallas import tpu as pltpu
from jax.sharding import Mesh, PartitionSpec as P

NEWTON = 2
ITERS = 3
PAIRS = 4
SAMPLES = 8
ROWS = 21
HELD = 24
SHRINK = 2.0**-10
VMEM = 48 * 1024 * 1024
FULL = 57 * 1024 * 1024


def shift_up(v, first):
    return jnp.where(first, 0.0, pltpu.roll(v, 1, 0))


def shift_down(v, last):
    return jnp.where(last, 0.0, pltpu.roll(v, v.shape[0] - 1, 0))


def edges(shape):
    row = lax.broadcasted_iota(jnp.int32, shape, 0)
    return row == 0, row == shape[0] - 1


def refine(v, taps, ends):
    even, odd = v
    return (
        taps[0] * shift_up(odd, ends[0]) + taps[1] * even + taps[2] * odd,
        taps[0] * even + taps[1] * odd + taps[2] * shift_down(even, ends[1]),
    )


def transpose_refine(u, taps, ends):
    even, odd = u
    return (
        taps[0] * odd + taps[1] * even + taps[2] * shift_up(odd, ends[0]),
        taps[0] * shift_down(even, ends[1]) + taps[1] * odd + taps[2] * even,
    )


def wide(column):
    return jnp.concatenate([column, column], axis=1)


def back(base, field, factors, weight, offset, taps, ends, scale):
    terms = []
    for p in range(2):
        w = base[p] if field is None else base[p] * field[p]
        total = None
        for k in range(SAMPLES):
            factor = factors[k, p]
            column = weight[p] * jnp.sum(factor * w, axis=1, keepdims=True)
            if offset is not None:
                column = column - offset[p]
            term = factor * wide(column)
            total = term if total is None else total + term
        terms.append(base[p] * total)
    return tuple(scale * t for t in transpose_refine(terms, taps, ends))


def dot(a, b):
    total = a[0] * b[0] + a[1] * b[1]
    total = jnp.sum(total[:, :128] + total[:, 128:], axis=0, keepdims=True)
    return jnp.sum(total, axis=1, keepdims=True)


def moments_row(basis):
    pairs = [(0, 0), (0, 1), (1, 1), (1, 2), (2, 2), (2, 3)]
    lane = lax.broadcasted_iota(jnp.int32, (1, 128), 1)
    row = jnp.zeros((1, 128), jnp.float32)
    for n, (i, j) in enumerate(pairs):
        row = jnp.where(lane == n, dot(basis[i], basis[j]), row)
    return row


def two_sum(a, b):
    total = a + b
    part = total - a
    return total, (a - (total - part)) + (b - part)


def halves_of(a):
    scaled = a * 4097.0
    high = scaled - (scaled - a)
    return high, a - high


def two_product(a, b):
    product = a * b
    (ah, al), (bh, bl) = halves_of(a), halves_of(b)
    return product, ((ah * bh - product) + ah * bl + al * bh) + al * bl


def careful_sum(rows):
    total, rest = rows[:8], jnp.zeros((8, 128), jnp.float32)
    for t in range(8, rows.shape[0], 8):
        total, error = two_sum(total, rows[t : t + 8])
        rest = rest + error
    for shift in (4, 2, 1):
        other, other_rest = pltpu.roll(total, shift, 0), pltpu.roll(rest, shift, 0)
        total, error = two_sum(total, other)
        rest = rest + other_rest + error
    return total[:1], rest[:1]


def coefficients(rows):
    lane = lax.broadcasted_iota(jnp.int32, (1, 128), 1)
    total, rest = careful_sum(rows)
    nu = [
        tuple(jnp.sum(jnp.where(lane == n, part, 0.0), axis=1, keepdims=True) for part in (total, rest))
        for n in range(2 * ITERS)
    ]
    zero, one = jnp.zeros((1, 1), jnp.float32), jnp.ones((1, 1), jnp.float32)

    def inner(a, b):
        weights = {}
        for i, x in enumerate(a):
            for j, y in enumerate(b):
                if i + j < 2 * ITERS:
                    product, error = two_product(x, y)
                    if i + j in weights:
                        high, low = weights[i + j]
                        high, more = two_sum(high, product)
                        weights[i + j] = high, low + (error + more)
                    else:
                        weights[i + j] = product, error
        total, rest = None, zero
        for n, (high, low) in weights.items():
            product, error = two_product(high, nu[n][0])
            error = error + (high * nu[n][1] + low * nu[n][0])
            if total is None:
                total, rest = product, error
            else:
                total, more = two_sum(total, product)
                rest = rest + (error + more)
        return total + rest

    def ratio(a, b):
        return jnp.where(b > 0.0, a / jnp.where(b > 0.0, b, 1.0), 0.0)

    residual = [one]
    direction = [one]
    step = [zero] * ITERS
    norm_now = nu[0][0] + nu[0][1]
    for it in range(ITERS):
        padded = direction + [zero]
        image = [padded[0]] + [padded[j] + (1.0 / SHRINK) * padded[j - 1] for j in range(1, len(padded))]
        alpha = jnp.clip(ratio(norm_now, inner(direction, image)), 0.0, 1.0)
        step = [s + alpha * direction[j] if j < len(direction) else s for j, s in enumerate(step)]
        residual = [r - alpha * i for r, i in zip(residual + [zero], image)]
        if it < ITERS - 1:
            norm_next = jnp.maximum(inner(residual, residual), 0.0)
            beta = ratio(norm_next, norm_now)
            direction = [r + beta * d for r, d in zip(residual, direction + [zero])]
            norm_now = norm_next
    return step, residual


def combine(coefs, basis):
    out = []
    for p in range(2):
        total = coefs[0] * basis[0][p]
        for c, b in zip(coefs[1:], basis[1:]):
            total = total + c * b[p]
        out.append(total)
    return tuple(out)


def krylov(latent, factors, weight, offset, taps, ends):
    base = tuple(jnp.exp(t) for t in refine(latent, taps, ends))
    pulled = back(base, None, factors, weight, offset, taps, ends, 1.0 / SAMPLES)
    basis = [tuple(-m - t for m, t in zip(latent, pulled))]
    for _ in range(ITERS):
        basis.append(
            back(base, refine(basis[-1], taps, ends), factors, weight, None, taps, ends, SHRINK / SAMPLES)
        )
    return basis


def pack_kernel(
    code, mean_all, draws_all, mask_all, noise_all, data_all, out,
    mean, draws, mask, noise, data, sems, *, count, members, copies, lines,
):
    first = pl.multiple_of((code[0] % members) * count, count)
    mine = pl.ds(first, count)
    loads = [
        pltpu.make_async_copy(source, target, sems.at[n])
        for n, (source, target) in enumerate(
            [
                (mean_all.at[:, mine, :], mean),
                (draws_all.at[:, :, mine, :], draws),
                (mask_all, mask),
                (noise_all, noise),
                (data_all, data),
            ]
        )
    ]
    for load in loads:
        load.start()
    for load in loads:
        load.wait()

    def place(r, rows):
        for fy in range(count // lines):
            for c in range(copies):
                first_block = (fy * copies + c) * lines
                out[pl.ds(first_block * ROWS + r, lines, stride=ROWS), :] = rows[fy * lines : fy * lines + lines]

    for a in range(1 + PAIRS):
        for p in range(2):
            for h in range(2):
                lanes = slice(h * 128, h * 128 + 128)
                rows = mean[p, :, lanes] if a == 0 else draws[a - 1, p, :, lanes]
                place(a * 4 + p * 2 + h, rows)
    row = lax.broadcasted_iota(jnp.int32, (count, 128), 0)
    lane = lax.broadcasted_iota(jnp.int32, (count, 128), 1)
    chosen = lane == row + first
    noisy = mask[...].astype(jnp.float32) * noise[...]
    extra = jnp.zeros((count, 128), jnp.float32)
    for n, values in enumerate((noisy * (1.0 / 256.0), noisy * data[...])):
        for p in range(2):
            picked = jnp.sum(jnp.where(chosen, values[p : p + 1, :], 0.0), axis=1, keepdims=True)
            extra = jnp.where(lane == n * 2 + p, picked, extra)
    place(20, extra)


def plane_rows(ref, a, p, n):
    return jnp.concatenate([ref[pl.ds(a * 4 + p * 2 + h, n, stride=ROWS), :] for h in range(2)], axis=1)


def columns(ref, n):
    extra = ref[pl.ds(20, n, stride=ROWS), :]
    spread = [jnp.broadcast_to(extra[:, c : c + 1], extra.shape) for c in range(4)]
    return spread[:2], spread[2:]


def first_kernel(packed, kernel, sums, factors, held, *, n):
    taps = [kernel[t : t + 1, :] for t in range(3)]
    ends = edges((n, 256))
    latent = tuple(plane_rows(packed, 0, p, n) for p in range(2))
    for k in range(PAIRS):
        spread = refine(tuple(plane_rows(packed, 1 + k, p, n) for p in range(2)), taps, ends)
        for p in range(2):
            factors[2 * k, p] = jnp.exp(spread[p])
            factors[2 * k + 1, p] = jnp.exp(-spread[p])
    weight, offset = columns(packed, n)
    basis = krylov(latent, factors, weight, offset, taps, ends)
    for p in range(2):
        held[0, p] = latent[p]
        for j in range(ITERS):
            held[1 + j, p] = basis[j][p]
    sums[...] = moments_row(basis)


def second_kernel(code, sums, packed, kernel, factors, held, out, block, *, n, groups, lines, members):
    taps = [kernel[t : t + 1, :] for t in range(3)]
    ends = edges((n, 256))
    step, _ = coefficients(sums[...])
    basis = [tuple(held[j, p] for p in range(2)) for j in range(1 + ITERS)]
    latent = combine([jnp.ones((1, 1), jnp.float32)] + step, basis)
    weight, offset = columns(packed, n)
    basis = krylov(latent, factors, weight, offset, taps, ends)
    for a, v in enumerate([latent] + basis):
        for p in range(2):
            for h in range(2):
                block[pl.ds(a * 4 + p * 2 + h, n, stride=HELD), :] = v[p][:, h * 128 : h * 128 + 128]
    for fy in range(groups):
        for zl in range(lines):
            start = (fy * (n // groups) + zl) * HELD + (code[0] // members) * (lines * HELD)
            to = (fy * lines + zl) * ROWS
            out[pl.ds(to, ROWS - 1), :] = block[pl.ds(pl.multiple_of(start, 8), ROWS - 1), :]
    row = jnp.broadcast_to(moments_row(basis), (groups * lines, 128))
    out[pl.ds(ROWS - 1, groups * lines, stride=ROWS), :] = row


def last_kernel(code, found, other, mean_final, cg_residual, *, chips, count):
    core = code[0] % 2
    n = chips * count
    sums = [ref[pl.ds(20, n, stride=ROWS), :] for ref in (found, other)]
    step, residual = coefficients(jnp.concatenate(sums, axis=0))
    for ref, owner in ((found, core), (other, 1 - core)):
        for x in range(chips):
            rows = pl.ds(pl.multiple_of((2 * x + owner) * count, count), count)
            for p in range(2):
                for h in range(2):
                    v = [
                        ref[pl.ds(x * ROWS + a * 4 + p * 2 + h, count, stride=chips * ROWS), :]
                        for a in range(2 + ITERS)
                    ]
                    latent = v[0]
                    for c, b in zip(step, v[1:]):
                        latent = latent + c * b
                    rest = residual[0] * v[1]
                    for c, b in zip(residual[1:], v[2:]):
                        rest = rest + c * b
                    mean_final[p, rows, h * 128 : h * 128 + 128] = latent
                    cg_residual[p, rows, h * 128 : h * 128 + 128] = rest


def local(mean_start, sample_draws, kernel, sight_mask, noise_weight, data):
    nx, nc, nfy, nzq, nzl = (lax.axis_size(a) for a in ("x", "core", "fy", "zq", "zl"))
    members = nx * nc
    fields = nfy * nzq * nzl
    lines = nfy * nzl
    count = mean_start.shape[1] // members
    depth = mean_start.shape[2]
    f32 = functools.partial(jax.ShapeDtypeStruct, dtype=jnp.float32)
    params = pltpu.CompilerParams(vmem_limit_bytes=VMEM)
    whole = pl.BlockSpec(memory_space=pltpu.VMEM)
    scalar = pl.BlockSpec(memory_space=pltpu.SMEM)
    code = lax.axis_index("zq") * members + lax.axis_index("x") * nc + lax.axis_index("core")
    code = code.astype(jnp.int32).reshape(1)

    packed = pl.pallas_call(
        functools.partial(pack_kernel, count=count, members=members, copies=nzq, lines=nzl),
        out_shape=f32((fields * ROWS, 128)),
        in_specs=[scalar] + [pl.BlockSpec(memory_space=pltpu.HBM)] * 5,
        out_specs=whole,
        scratch_shapes=[
            pltpu.VMEM((2, count, depth), jnp.float32),
            pltpu.VMEM((PAIRS, 2, count, depth), jnp.float32),
            pltpu.VMEM(sight_mask.shape, jnp.int32),
            pltpu.VMEM(noise_weight.shape, jnp.float32),
            pltpu.VMEM(data.shape, jnp.float32),
            pltpu.SemaphoreType.DMA((5,)),
        ],
        compiler_params=pltpu.CompilerParams(vmem_limit_bytes=FULL),
        name="pack",
    )(code, mean_start, sample_draws, sight_mask, noise_weight, data)

    packed = lax.all_to_all(packed.reshape(fields * ROWS, 1, 128), ("fy", "zq", "zl"), 0, 0, tiled=True)
    packed = packed.reshape(fields * ROWS, 128)

    sharers = members * lines
    sums, factors, held = pl.pallas_call(
        functools.partial(first_kernel, n=fields),
        out_shape=[
            f32((1, 128)),
            f32((SAMPLES, 2, fields, depth)),
            f32((1 + ITERS, 2, fields, depth)),
        ],
        in_specs=[whole, whole],
        out_specs=[whole, whole, whole],
        compiler_params=params,
        name="first",
    )(packed, kernel)

    sums = jnp.broadcast_to(sums[None], (sharers, 1, 128))
    sums = lax.all_to_all(sums, ("core", "x", "fy", "zl"), 0, 0, tiled=True)
    sums = sums.reshape(sharers, 128)

    found = pl.pallas_call(
        functools.partial(second_kernel, n=fields, groups=nfy, lines=nzl, members=members),
        out_shape=f32((lines * ROWS, 128)),
        in_specs=[scalar] + [whole] * 5,
        out_specs=whole,
        scratch_shapes=[pltpu.VMEM((fields * HELD, 128), jnp.float32)],
        compiler_params=params,
        name="second",
    )(code, sums, packed, kernel, factors, held)

    found = jnp.broadcast_to(found.reshape(lines, 1, ROWS, 1, 128), (lines, nx, ROWS, 1, 128))
    found = lax.all_to_all(found.reshape(lines * nx * ROWS, 1, 128), ("fy", "zl", "x"), 0, 0, tiled=True)
    found = found.reshape(nx * lines * ROWS, 128)
    other = lax.ppermute(found, "core", [(0, 1), (1, 0)])

    return pl.pallas_call(
        functools.partial(last_kernel, chips=nx, count=count),
        out_shape=[f32(mean_start.shape), f32(mean_start.shape)],
        in_specs=[scalar, whole, whole],
        out_specs=[whole, whole],
        compiler_params=params,
        name="last",
    )(code, found, other)


def solution(mesh):
    split = Mesh(mesh.devices.reshape(4, 2, 4, 4, 4), ("x", "core", "fy", "zq", "zl"))
    field = ("fy", "zq", "zl")
    placed = (
        P(field, None, None),
        P(None, field, None, None),
        P(),
        P(field, None),
        P(field, None),
        P(field, None),
    )
    return jax.shard_map(
        local,
        mesh=split,
        in_specs=placed,
        out_specs=(P(field, None, None), P(field, None, None)),
        check_vma=False,
    )
```

```python
import functools

import jax
import jax.numpy as jnp
from jax import lax
from jax.experimental import pallas as pl
from jax.experimental.pallas import tpu as pltpu
from jax.sharding import Mesh, PartitionSpec as P

NEWTON = 2
ITERS = 3
PAIRS = 4
SAMPLES = 8
ROWS = 21
HELD = 24
SHRINK = 2.0**-10
VMEM = 48 * 1024 * 1024
FULL = 57 * 1024 * 1024


def shift_up(v, first):
    return jnp.where(first, 0.0, pltpu.roll(v, 1, 0))


def shift_down(v, last):
    return jnp.where(last, 0.0, pltpu.roll(v, v.shape[0] - 1, 0))


def edges(shape):
    row = lax.broadcasted_iota(jnp.int32, shape, 0)
    return row == 0, row == shape[0] - 1


def refine(v, taps, ends):
    even, odd = v
    return (
        taps[0] * shift_up(odd, ends[0]) + taps[1] * even + taps[2] * odd,
        taps[0] * even + taps[1] * odd + taps[2] * shift_down(even, ends[1]),
    )


def transpose_refine(u, taps, ends):
    even, odd = u
    return (
        taps[0] * odd + taps[1] * even + taps[2] * shift_up(odd, ends[0]),
        taps[0] * shift_down(even, ends[1]) + taps[1] * odd + taps[2] * even,
    )


def wide(column):
    return jnp.concatenate([column, column], axis=1)


def back(base, field, factors, weight, offset, taps, ends, scale):
    terms = []
    for p in range(2):
        w = base[p] if field is None else base[p] * field[p]
        total = None
        for k in range(SAMPLES):
            factor = factors[k, p]
            column = weight[p] * jnp.sum(factor * w, axis=1, keepdims=True)
            if offset is not None:
                column = column - offset[p]
            term = factor * wide(column)
            total = term if total is None else total + term
        terms.append(base[p] * total)
    return tuple(scale * t for t in transpose_refine(terms, taps, ends))


def dot(a, b):
    total = a[0] * b[0] + a[1] * b[1]
    total = jnp.sum(total[:, :128] + total[:, 128:], axis=0, keepdims=True)
    return jnp.sum(total, axis=1, keepdims=True)


def moments_row(basis):
    pairs = [(0, 0), (0, 1), (1, 1), (1, 2), (2, 2), (2, 3)]
    lane = lax.broadcasted_iota(jnp.int32, (1, 128), 1)
    row = jnp.zeros((1, 128), jnp.float32)
    for n, (i, j) in enumerate(pairs):
        row = jnp.where(lane == n, dot(basis[i], basis[j]), row)
    return row


def two_sum(a, b):
    total = a + b
    part = total - a
    return total, (a - (total - part)) + (b - part)


def halves_of(a):
    scaled = a * 4097.0
    high = scaled - (scaled - a)
    return high, a - high


def two_product(a, b):
    product = a * b
    (ah, al), (bh, bl) = halves_of(a), halves_of(b)
    return product, ((ah * bh - product) + ah * bl + al * bh) + al * bl


def careful_sum(rows):
    total, rest = rows[:8], jnp.zeros((8, 128), jnp.float32)
    for t in range(8, rows.shape[0], 8):
        total, error = two_sum(total, rows[t : t + 8])
        rest = rest + error
    for shift in (4, 2, 1):
        other, other_rest = pltpu.roll(total, shift, 0), pltpu.roll(rest, shift, 0)
        total, error = two_sum(total, other)
        rest = rest + other_rest + error
    return total[:1], rest[:1]


def coefficients(rows):
    lane = lax.broadcasted_iota(jnp.int32, (1, 128), 1)
    total, rest = careful_sum(rows)
    nu = [
        tuple(jnp.sum(jnp.where(lane == n, part, 0.0), axis=1, keepdims=True) for part in (total, rest))
        for n in range(2 * ITERS)
    ]
    zero, one = jnp.zeros((1, 1), jnp.float32), jnp.ones((1, 1), jnp.float32)

    def inner(a, b):
        weights = {}
        for i, x in enumerate(a):
            for j, y in enumerate(b):
                if i + j < 2 * ITERS:
                    product, error = two_product(x, y)
                    if i + j in weights:
                        high, low = weights[i + j]
                        high, more = two_sum(high, product)
                        weights[i + j] = high, low + (error + more)
                    else:
                        weights[i + j] = product, error
        total, rest = None, zero
        for n, (high, low) in weights.items():
            product, error = two_product(high, nu[n][0])
            error = error + (high * nu[n][1] + low * nu[n][0])
            if total is None:
                total, rest = product, error
            else:
                total, more = two_sum(total, product)
                rest = rest + (error + more)
        return total + rest

    def ratio(a, b):
        return jnp.where(b > 0.0, a / jnp.where(b > 0.0, b, 1.0), 0.0)

    residual = [one]
    direction = [one]
    step = [zero] * ITERS
    norm_now = nu[0][0] + nu[0][1]
    for it in range(ITERS):
        padded = direction + [zero]
        image = [padded[0]] + [padded[j] + (1.0 / SHRINK) * padded[j - 1] for j in range(1, len(padded))]
        alpha = jnp.clip(ratio(norm_now, inner(direction, image)), 0.0, 1.0)
        step = [s + alpha * direction[j] if j < len(direction) else s for j, s in enumerate(step)]
        residual = [r - alpha * i for r, i in zip(residual + [zero], image)]
        if it < ITERS - 1:
            norm_next = jnp.maximum(inner(residual, residual), 0.0)
            beta = ratio(norm_next, norm_now)
            direction = [r + beta * d for r, d in zip(residual, direction + [zero])]
            norm_now = norm_next
    return step, residual


def combine(coefs, basis):
    out = []
    for p in range(2):
        total = coefs[0] * basis[0][p]
        for c, b in zip(coefs[1:], basis[1:]):
            total = total + c * b[p]
        out.append(total)
    return tuple(out)


def krylov(latent, factors, weight, offset, taps, ends):
    base = tuple(jnp.exp(t) for t in refine(latent, taps, ends))
    pulled = back(base, None, factors, weight, offset, taps, ends, 1.0 / SAMPLES)
    basis = [tuple(-m - t for m, t in zip(latent, pulled))]
    for _ in range(ITERS):
        basis.append(
            back(base, refine(basis[-1], taps, ends), factors, weight, None, taps, ends, SHRINK / SAMPLES)
        )
    return basis


def pack_kernel(
    code, mean_all, draws_all, mask_all, noise_all, data_all, out,
    mean, draws, mask, noise, data, sems, *, count, members, copies, lines,
):
    first = pl.multiple_of((code[0] % members) * count, count)
    mine = pl.ds(first, count)
    loads = [
        pltpu.make_async_copy(source, target, sems.at[n])
        for n, (source, target) in enumerate(
            [
                (mean_all.at[:, mine, :], mean),
                (draws_all.at[:, :, mine, :], draws),
                (mask_all, mask),
                (noise_all, noise),
                (data_all, data),
            ]
        )
    ]
    for load in loads:
        load.start()
    for load in loads:
        load.wait()

    def place(r, rows):
        for fy in range(count // lines):
            for c in range(copies):
                first_block = (fy * copies + c) * lines
                out[pl.ds(first_block * ROWS + r, lines, stride=ROWS), :] = rows[fy * lines : fy * lines + lines]

    for a in range(1 + PAIRS):
        for p in range(2):
            for h in range(2):
                lanes = slice(h * 128, h * 128 + 128)
                rows = mean[p, :, lanes] if a == 0 else draws[a - 1, p, :, lanes]
                place(a * 4 + p * 2 + h, rows)
    row = lax.broadcasted_iota(jnp.int32, (count, 128), 0)
    lane = lax.broadcasted_iota(jnp.int32, (count, 128), 1)
    chosen = lane == row + first
    noisy = mask[...].astype(jnp.float32) * noise[...]
    extra = jnp.zeros((count, 128), jnp.float32)
    for n, values in enumerate((noisy * (1.0 / 256.0), noisy * data[...])):
        for p in range(2):
            picked = jnp.sum(jnp.where(chosen, values[p : p + 1, :], 0.0), axis=1, keepdims=True)
            extra = jnp.where(lane == n * 2 + p, picked, extra)
    place(20, extra)


def plane_rows(ref, a, p, n):
    return jnp.concatenate([ref[pl.ds(a * 4 + p * 2 + h, n, stride=ROWS), :] for h in range(2)], axis=1)


def columns(ref, n):
    extra = ref[pl.ds(20, n, stride=ROWS), :]
    spread = [jnp.broadcast_to(extra[:, c : c + 1], extra.shape) for c in range(4)]
    return spread[:2], spread[2:]


def first_kernel(packed, kernel, sums, factors, held, *, n):
    taps = [kernel[t : t + 1, :] for t in range(3)]
    ends = edges((n, 256))
    latent = tuple(plane_rows(packed, 0, p, n) for p in range(2))
    for k in range(PAIRS):
        spread = refine(tuple(plane_rows(packed, 1 + k, p, n) for p in range(2)), taps, ends)
        for p in range(2):
            grown = jnp.exp(spread[p])
            factors[2 * k, p] = grown
            factors[2 * k + 1, p] = 1.0 / grown
    weight, offset = columns(packed, n)
    basis = krylov(latent, factors, weight, offset, taps, ends)
    for p in range(2):
        held[0, p] = latent[p]
        for j in range(ITERS):
            held[1 + j, p] = basis[j][p]
    sums[...] = moments_row(basis)


def second_kernel(code, sums, packed, kernel, factors, held, out, block, *, n, groups, lines, members):
    taps = [kernel[t : t + 1, :] for t in range(3)]
    ends = edges((n, 256))
    step, _ = coefficients(sums[...])
    basis = [tuple(held[j, p] for p in range(2)) for j in range(1 + ITERS)]
    latent = combine([jnp.ones((1, 1), jnp.float32)] + step, basis)
    weight, offset = columns(packed, n)
    basis = krylov(latent, factors, weight, offset, taps, ends)
    for a, v in enumerate([latent] + basis):
        for p in range(2):
            for h in range(2):
                block[pl.ds(a * 4 + p * 2 + h, n, stride=HELD), :] = v[p][:, h * 128 : h * 128 + 128]
    for fy in range(groups):
        for zl in range(lines):
            start = (fy * (n // groups) + zl) * HELD + (code[0] // members) * (lines * HELD)
            to = (fy * lines + zl) * ROWS
            out[pl.ds(to, ROWS - 1), :] = block[pl.ds(pl.multiple_of(start, 8), ROWS - 1), :]
    row = jnp.broadcast_to(moments_row(basis), (groups * lines, 128))
    out[pl.ds(ROWS - 1, groups * lines, stride=ROWS), :] = row


def last_kernel(code, found, other, mean_final, cg_residual, *, chips, count):
    core = code[0] % 2
    n = chips * count
    sums = [ref[pl.ds(20, n, stride=ROWS), :] for ref in (found, other)]
    step, residual = coefficients(jnp.concatenate(sums, axis=0))
    for ref, owner in ((found, core), (other, 1 - core)):
        for x in range(chips):
            rows = pl.ds(pl.multiple_of((2 * x + owner) * count, count), count)
            for p in range(2):
                for h in range(2):
                    v = [
                        ref[pl.ds(x * count * ROWS + a * 4 + p * 2 + h, count, stride=ROWS), :]
                        for a in range(2 + ITERS)
                    ]
                    latent = v[0]
                    for c, b in zip(step, v[1:]):
                        latent = latent + c * b
                    rest = residual[0] * v[1]
                    for c, b in zip(residual[1:], v[2:]):
                        rest = rest + c * b
                    mean_final[p, rows, h * 128 : h * 128 + 128] = latent
                    cg_residual[p, rows, h * 128 : h * 128 + 128] = rest


def spread(block, axis):
    copies = lax.axis_size(axis)
    block = jnp.broadcast_to(block[None], (copies,) + block.shape)
    return lax.all_to_all(block, axis, 0, 0, tiled=True)


def local(mean_start, sample_draws, kernel, sight_mask, noise_weight, data):
    nx, nc, nfy, nzq, nzl = (lax.axis_size(a) for a in ("x", "core", "fy", "zq", "zl"))
    members = nx * nc
    fields = nfy * nzq * nzl
    lines = nfy * nzl
    count = mean_start.shape[1] // members
    depth = mean_start.shape[2]
    f32 = functools.partial(jax.ShapeDtypeStruct, dtype=jnp.float32)
    params = pltpu.CompilerParams(vmem_limit_bytes=VMEM)
    whole = pl.BlockSpec(memory_space=pltpu.VMEM)
    scalar = pl.BlockSpec(memory_space=pltpu.SMEM)
    code = lax.axis_index("zq") * members + lax.axis_index("x") * nc + lax.axis_index("core")
    code = code.astype(jnp.int32).reshape(1)

    packed = pl.pallas_call(
        functools.partial(pack_kernel, count=count, members=members, copies=nzq, lines=nzl),
        out_shape=f32((fields * ROWS, 128)),
        in_specs=[scalar] + [pl.BlockSpec(memory_space=pltpu.HBM)] * 5,
        out_specs=whole,
        scratch_shapes=[
            pltpu.VMEM((2, count, depth), jnp.float32),
            pltpu.VMEM((PAIRS, 2, count, depth), jnp.float32),
            pltpu.VMEM(sight_mask.shape, jnp.int32),
            pltpu.VMEM(noise_weight.shape, jnp.float32),
            pltpu.VMEM(data.shape, jnp.float32),
            pltpu.SemaphoreType.DMA((5,)),
        ],
        compiler_params=pltpu.CompilerParams(vmem_limit_bytes=FULL),
        name="pack",
    )(code, mean_start, sample_draws, sight_mask, noise_weight, data)

    packed = lax.all_to_all(packed.reshape(fields * ROWS, 1, 128), ("fy", "zq", "zl"), 0, 0, tiled=True)
    packed = packed.reshape(fields * ROWS, 128)

    sharers = members * lines
    sums, factors, held = pl.pallas_call(
        functools.partial(first_kernel, n=fields),
        out_shape=[
            f32((1, 128)),
            f32((SAMPLES, 2, fields, depth)),
            f32((1 + ITERS, 2, fields, depth)),
        ],
        in_specs=[whole, whole],
        out_specs=[whole, whole, whole],
        compiler_params=params,
        name="first",
    )(packed, kernel)

    sums = jnp.broadcast_to(sums[None], (sharers, 1, 128))
    sums = lax.all_to_all(sums, ("core", "x", "fy", "zl"), 0, 0, tiled=True)
    sums = sums.reshape(sharers, 128)

    found = pl.pallas_call(
        functools.partial(second_kernel, n=fields, groups=nfy, lines=nzl, members=members),
        out_shape=f32((lines * ROWS, 128)),
        in_specs=[scalar] + [whole] * 5,
        out_specs=whole,
        scratch_shapes=[pltpu.VMEM((fields * HELD, 128), jnp.float32)],
        compiler_params=params,
        name="second",
    )(code, sums, packed, kernel, factors, held)

    found = lax.all_to_all(found.reshape(lines * ROWS, 1, 128), ("fy", "zl"), 0, 0, tiled=True)
    found = spread(found, "x").reshape(nx * lines * ROWS, 128)
    other = lax.ppermute(found, "core", [(0, 1), (1, 0)])

    return pl.pallas_call(
        functools.partial(last_kernel, chips=nx, count=count),
        out_shape=[f32(mean_start.shape), f32(mean_start.shape)],
        in_specs=[scalar, whole, whole],
        out_specs=[whole, whole],
        compiler_params=params,
        name="last",
    )(code, found, other)


def solution(mesh):
    split = Mesh(mesh.devices.reshape(4, 2, 4, 4, 4), ("x", "core", "fy", "zq", "zl"))
    field = ("fy", "zq", "zl")
    placed = (
        P(field, None, None),
        P(None, field, None, None),
        P(),
        P(field, None),
        P(field, None),
        P(field, None),
    )
    return jax.shard_map(
        local,
        mesh=split,
        in_specs=placed,
        out_specs=(P(field, None, None), P(field, None, None)),
        check_vma=False,
    )
```
